32 devices in a mesh: dp: 8 (over z, core), fsdp: 4 (over y, x).
Axes of the slice: x: 2, y: 2, z: 4, core: 2. Of those that a mesh axis runs over, the one named last changes fastest.
Arguments:
- acts: bfloat16 [8192, 4096], P(('dp', 'fsdp')), may hold values from -6 to 6
- cotangent: bfloat16 [8192, 4096], P(('dp', 'fsdp')), may hold values from -0.3125 to 0.3125
- projector: bfloat16 [4096, 512], P('fsdp'), may hold values from -0.09375 to 0.09375
- first_moment: float32 [4096, 512], P('fsdp'), may hold values from -4 to 4
- second_moment: float32 [4096, 512], P('fsdp'), may hold values from 0.0005 to 0.005
Outputs:
- first_new: float32 [4096, 512], P('fsdp')
- second_new: float32 [4096, 512], P('fsdp')
- update: float32 [4096, 4096], P(None, 'fsdp')
The draws below stay inside these ranges and needn't reach their ends.
All inputs are finite; a program needn't handle non-finite values.
Results may differ from the reference program's by a relative error of at most 0.017.
Values may be sent and summed in bfloat16 or wider, within the bound.
No kernel may reach another device: no remote copies, remote signals or barrier semaphores. Data moves between devices by JAX's collectives and lax.ppermute only.
A program may use at most 128 MiB of HBM per device.

```python
import math
import jax
import jax.numpy as jnp
from jax import lax

D = 4096
RANK = 512
TOK_DEV = 256
STEP = 2
TOKENS = 8192


def with_spikes(array, own_key, source, target, parts, factor):
    owner, partner = [(jnp.arange(array.shape[dim]) // (array.shape[dim] // parts)).reshape([-1 if axis == dim else 1 for axis in range(array.ndim)]) for dim in (source, target)]
    chosen = jax.random.permutation(own_key, parts)[partner]
    strong = (owner == chosen) | (owner == (partner + parts // 2) % parts)
    return jnp.where(strong, factor * array, array)


def block_levels(key, extent, cuts, least, high):
    factor_of = 1.0
    for axis_at, parts in cuts:
        steps = jax.random.uniform(jax.random.fold_in(jax.random.fold_in(key, 6), axis_at), (parts,), jnp.float32, least / len(cuts), high / len(cuts))
        factor_of = factor_of * jnp.repeat(jnp.exp(steps), extent[axis_at] // parts).reshape((-1,) + (1,) * (len(extent) - 1 - axis_at))
    return factor_of


def gaussian(own_key, shape, scale, reach, shards=(), dtype=jnp.bfloat16):
    entries = jax.random.normal(own_key, shape, jnp.float32) * scale
    if len(shards) > 0:
        entries = block_levels(own_key, shape, shards, -0.22, 0.18) * entries
    return jnp.clip(entries, min=-reach, max=reach).astype(dtype)


def gaussian_with(rng, dims, width, most, split, heavy, kind=jnp.bfloat16):
    entries = width * jax.random.normal(rng, dims, jnp.float32)
    if split:
        entries = entries * block_levels(rng, dims, split, -0.22, 0.18)
    return jnp.clip(with_spikes(entries, jax.random.fold_in(rng, 3), *heavy), -most, most).astype(kind)


def setup_inputs(seed: int = 0) -> dict:
    seeds = jax.random.split(jax.random.key(seed), 6)
    acts = gaussian(seeds[0], (TOKENS, D), 1.0, 6.0, ((0, 32),))
    cotangent = gaussian_with(seeds[1], (TOKENS, D), (TOKENS ** -0.5), 0.3125, ((0, 32),), (0, 1, 32, 2.75))
    projector = gaussian(seeds[2], (D, RANK), D ** -0.5, 0.09375, ((0, 4),))
    first_moment = gaussian(seeds[3], (D, RANK), 0.3, 4.0, ((0, 4),), jnp.float32)
    second_moment = jnp.clip(jnp.exp(math.log(0.005) - 2.30258502 * jax.random.uniform(seeds[4], (D, RANK), jnp.float32) ** block_levels(seeds[4], (D, RANK), ((0, 4),), -0.2, 0.2)), 0.0005, 0.005)
    return dict(acts=acts, cotangent=cotangent, projector=projector, first_moment=first_moment, second_moment=second_moment)


def reference(acts, cotangent, projector, first_moment, second_moment):
    blocks = TOKENS // TOK_DEV
    acts_blocks = acts.reshape(blocks, TOK_DEV, D)
    cot_blocks = cotangent.reshape(blocks, TOK_DEV, D)
    proj_wide = projector.astype(jnp.float32)

    def accumulate(total, pair):
        block_acts, block_cot = pair
        coords = jnp.dot(block_acts.astype(jnp.float32), proj_wide, preferred_element_type=jnp.float32).astype(jnp.bfloat16)
        term = jnp.dot(block_cot.astype(jnp.float32).T, coords.astype(jnp.float32), preferred_element_type=jnp.float32)
        term = lax.optimization_barrier(term.astype(jnp.bfloat16)).astype(jnp.float32)
        return (total + term, None)
    grad_low, _ = lax.scan(accumulate, jnp.zeros((D, RANK), jnp.float32), (acts_blocks, cot_blocks))
    first_new = 0.9 * first_moment + 0.1 * grad_low
    second_new = 0.999 * second_moment + 0.001 * grad_low * grad_low
    first_fix = 1.0 - 0.9 ** STEP
    second_fix = 1.0 - 0.999 ** STEP
    direction = (first_new / first_fix / (jnp.sqrt(second_new / second_fix) + 1e-08)).astype(jnp.bfloat16)
    update = lax.dot_general(projector, direction, (((1,), (1,)), ((), ())), preferred_element_type=jnp.float32)
    return (first_new, second_new, update)
```

```python
import functools

import jax
import jax.numpy as jnp
from jax import lax
from jax.experimental import pallas as pl
from jax.experimental.pallas import tpu as pltpu
from jax.sharding import PartitionSpec as P

STEP = 2
CORES = 2
CHUNKS = 2
MIB = 1024 * 1024
BF16 = jnp.bfloat16
F32 = jnp.float32


def cost(flops, bytes_accessed):
    return pl.CostEstimate(flops=flops, bytes_accessed=bytes_accessed, transcendentals=0)


def whole(array):
    zeros = (0,) * array.ndim
    return pl.BlockSpec(array.shape, lambda i, w: zeros)


def call(body, where, inputs, in_specs, out_shape, limit, scratch=(), name=None, estimate=None):
    return pl.pallas_call(
        body,
        out_shape=out_shape,
        grid_spec=pltpu.PrefetchScalarGridSpec(
            num_scalar_prefetch=1,
            grid=(1,),
            in_specs=in_specs,
            out_specs=[whole(x) for x in out_shape],
            scratch_shapes=scratch,
        ),
        compiler_params=pltpu.CompilerParams(vmem_limit_bytes=limit),
        cost_estimate=estimate,
        name=name,
    )(where, *inputs)


def own_columns(where, projector):
    rows, rank = projector.shape
    half = rank // CORES

    def body(w, x_ref, y_ref, sem):
        columns = pl.ds(pl.multiple_of(w[1] * half, half), half)
        copy = pltpu.make_async_copy(x_ref.at[:, columns], y_ref, sem)
        copy.start()
        copy.wait()

    return pl.pallas_call(
        body,
        out_shape=jax.ShapeDtypeStruct((rows, half), BF16),
        in_specs=[
            pl.BlockSpec(memory_space=pltpu.SMEM),
            pl.BlockSpec(memory_space=pltpu.HBM),
        ],
        out_specs=pl.BlockSpec(memory_space=pltpu.VMEM),
        scratch_shapes=[pltpu.SemaphoreType.DMA],
        compiler_params=pltpu.CompilerParams(vmem_limit_bytes=4 * MIB),
        cost_estimate=cost(0, 4 * rows * half),
        name="own_columns",
    )(where, projector)


def stage(where, acts, cots, proj, total, coords, terms, rows, last, name):
    tokens = cots[0].shape[0]
    half = proj[0][2].shape[1] if proj else coords.shape[0]
    inputs, specs, out_shape = [], [], []

    def add(array, spec):
        inputs.append(array)
        specs.append(spec)

    for s, low, block in proj:
        size = block.shape[0]
        at = functools.partial(
            lambda s, low, size, i, w: (0, ((w[0] ^ s) * rows + low) // size), s, low, size
        )
        for x in acts:
            add(x, pl.BlockSpec((tokens, size), at))
        add(block, whole(block))
    if total is not None:
        add(total, whole(total))
    if coords is not None:
        add(coords, whole(coords))
    for s, j, chunk, added, pieces, cuts in terms:
        at = functools.partial(
            lambda s, j, chunk, i, w: (0, (w[0] ^ s) * (rows // chunk) + j), s, j, chunk
        )
        for x in cots:
            add(x, pl.BlockSpec((tokens, chunk), at))
        for _, x in added:
            at = functools.partial(lambda j, i, w: (0, j), j if x.shape[1] > chunk else 0)
            add(x, pl.BlockSpec((x.shape[0], chunk), at))
    if last:
        out_shape.append(jax.ShapeDtypeStruct((half, 2 * tokens), BF16))
    elif proj:
        out_shape.append(jax.ShapeDtypeStruct((2 * tokens, half), F32))
    widest = 128
    for _, _, chunk, _, pieces, cuts in terms:
        widest = max(widest, chunk)
        for a, b in cuts:
            out_shape += [jax.ShapeDtypeStruct((b - a, chunk // pieces), BF16)] * pieces

    def body(w, *refs):
        ins = iter(refs[: len(inputs)])
        outs = iter(refs[len(inputs) : len(inputs) + len(out_shape)])
        value = refs[-1]
        if proj:
            sums = [None, None]
            for _ in proj:
                a, b, block = next(ins), next(ins), next(ins)
                for t, x in enumerate((a, b)):
                    part = jnp.dot(x[...], block[...], preferred_element_type=F32)
                    sums[t] = part if sums[t] is None else sums[t] + part
            if total is not None:
                before = next(ins)
                sums = [x + before[t * tokens : (t + 1) * tokens, :] for t, x in enumerate(sums)]
            out = next(outs)
            for t, x in enumerate(sums):
                span = slice(t * tokens, (t + 1) * tokens)
                if last:
                    out[:, span] = x.T.astype(BF16)
                else:
                    out[span, :] = x
            coords_ref = out
        if coords is not None:
            coords_ref = next(ins)
        for _, _, chunk, added, pieces, cuts in terms:
            a, b = next(ins), next(ins)
            term = jnp.dot(coords_ref[:, :tokens], a[...], preferred_element_type=F32)
            term += jnp.dot(coords_ref[:, tokens:], b[...], preferred_element_type=F32)
            value[:, :chunk] = term
            for low, x in added:
                ref = next(ins)
                value[low : low + x.shape[0], :chunk] += ref[...].astype(F32)
            size = chunk // pieces
            for a, b in cuts:
                for k in range(pieces):
                    at = 0
                    if pieces > 1:
                        at = pl.multiple_of(lax.rem(w[2] + k, pieces) * size, size)
                    next(outs)[...] = value[a:b, pl.ds(at, size)].astype(BF16)

    flops = sum(4 * tokens * half * x[2].shape[0] for x in proj)
    flops += sum(4 * tokens * half * x[2] for x in terms)
    return call(
        body,
        where,
        inputs,
        specs,
        out_shape,
        20 * MIB,
        scratch=[pltpu.VMEM((half, widest), F32)],
        name=name,
        estimate=cost(flops, flops // (2 * half)),
    )


def assemble(where, projector, own, other, rows):
    half = own[0][2].shape[1]
    parts = sum(x[2].shape[0] for x in own) // rows
    inputs = [projector] + [x for _, _, x in own + other]

    def body(w, *refs):
        ins, out = refs[:-1], refs[-1]
        out[pl.ds(pl.multiple_of(w[0] * rows, rows), rows), :] = ins[0][...]
        blocks = ins[1:]
        for n, (s, low, x) in enumerate(own):
            if s == 0:
                continue
            size = x.shape[0]
            at = pl.ds(pl.multiple_of((w[0] ^ s) * rows + low, size), size)
            mine, others = blocks[n], blocks[len(own) + n]

            @pl.when(w[1] == 0)
            def _():
                out[at, :half] = mine[...]
                out[at, half:] = others[...]

            @pl.when(w[1] != 0)
            def _():
                out[at, :half] = others[...]
                out[at, half:] = mine[...]

    shape = (parts * rows, 2 * half)
    return call(
        body,
        where,
        inputs,
        [whole(x) for x in inputs],
        [jax.ShapeDtypeStruct(shape, BF16)],
        28 * MIB,
        name="assemble",
        estimate=cost(0, 8 * parts * rows * half),
    )[0]


def update_step(where, j, k, pieces, own_grad, other_grad, proj, first, second, before):
    half, chunk = own_grad.shape
    rank = CORES * half
    features = first.shape[0]
    width = proj.shape[0]
    rows = min(512, width)

    def column(w):
        return j * pieces + lax.rem(w[2] + pieces - k, pieces)

    moment_block = pl.BlockSpec((chunk, rank), lambda i, w: (column(w), 0))

    def body(w, own_ref, other_ref, proj_ref, first_ref, second_ref, *refs):
        first_out, second_out, update, grad, direction = refs[-5:]

        @pl.when(pl.program_id(0) == 0)
        def _():
            at = pl.multiple_of(w[1] * half, half)
            grad[pl.ds(at, half), :] = own_ref[...].astype(F32)
            at = pl.multiple_of((1 - w[1]) * half, half)
            grad[pl.ds(at, half), :] = other_ref[...].astype(F32)
            grad_low = grad[...].T
            first_new = 0.9 * first_ref[...] + 0.1 * grad_low
            second_new = 0.999 * second_ref[...] + 0.001 * grad_low * grad_low
            first_out[...] = first_new
            second_out[...] = second_new
            first_fix = 1.0 - 0.9**STEP
            second_fix = 1.0 - 0.999**STEP
            ratio = first_new / first_fix / (jnp.sqrt(second_new / second_fix) + 1e-08)
            direction[...] = ratio.T.astype(BF16)

        update[...] = jnp.dot(proj_ref[...], direction[...], preferred_element_type=F32)

    inputs = [own_grad, other_grad, proj, first, second]
    in_specs = [whole(own_grad), whole(other_grad)]
    in_specs += [pl.BlockSpec((rows, rank), lambda i, w: (i, 0)), moment_block, moment_block]
    aliases = {}
    if before is not None:
        aliases = {1 + len(inputs) + n: n for n in range(3)}
        inputs += before
        in_specs += [pl.BlockSpec(memory_space=pl.ANY)] * 3
    return pl.pallas_call(
        body,
        out_shape=[
            jax.ShapeDtypeStruct(first.shape, F32),
            jax.ShapeDtypeStruct(second.shape, F32),
            jax.ShapeDtypeStruct((width, features), F32),
        ],
        grid_spec=pltpu.PrefetchScalarGridSpec(
            num_scalar_prefetch=1,
            grid=(width // rows,),
            in_specs=in_specs,
            out_specs=[moment_block, moment_block]
            + [pl.BlockSpec((rows, chunk), lambda i, w: (i, column(w)))],
            scratch_shapes=[pltpu.VMEM((rank, chunk), F32), pltpu.VMEM((rank, chunk), BF16)],
        ),
        input_output_aliases=aliases,
        compiler_params=pltpu.CompilerParams(vmem_limit_bytes=20 * MIB),
        cost_estimate=cost(2 * width * rank * chunk, 4 * width * chunk + 18 * chunk * rank),
        name="update_step",
    )(where, *inputs)


def add_up(arrays):
    return functools.reduce(jnp.add, [x.astype(F32) for x in arrays]).astype(BF16)


def on_device(dp, fsdp, acts, cotangent, projector, first_moment, second_moment):
    rows, rank = projector.shape
    half = rank // CORES
    groups = dp // CORES
    chunks = CHUNKS if rows % (256 * CHUNKS) == 0 else 1
    chunk = rows // chunks
    pieces = 2 if groups % 2 == 0 and chunk % 256 == 0 else 1
    fsdp_at = lax.axis_index("fsdp")
    dp_at = lax.axis_index("dp")
    where = jnp.stack([fsdp_at, dp_at % CORES, (dp_at // CORES) % pieces]).astype(jnp.int32)

    def to_core(x):
        return lax.ppermute(x, "dp", [(i, i ^ 1) for i in range(dp)])

    def to_fsdp(x, s):
        return lax.ppermute(x, "fsdp", [(i, i ^ s) for i in range(fsdp)])

    def to_piece(x, k):
        pairs = []
        for i in range(dp):
            group, core = divmod(i, CORES)
            base = group - group % pieces
            pairs.append((i, (base + (group + k) % pieces) * CORES + core))
        return lax.ppermute(x, "dp", pairs)

    def to_base(x, k):
        return lax.ppermute(x, "dp", [(i, (i + k * pieces * CORES) % dp) for i in range(dp)])

    def links(s):
        return (s & -s, 1 << (s.bit_length() - 1))

    levels = [
        [s for s in range(fsdp) if s.bit_count() == n] for n in range(fsdp.bit_length())
    ]

    own_half = own_columns(where, projector)
    held = {0: [(0, 0, own_half)]}
    for level in levels[1:]:
        for s in level:
            if s.bit_count() == 1:
                held[s] = [(s, 0, to_fsdp(own_half, s))]
                continue
            held[s] = []
            for n, link in enumerate(links(s)):
                source = held[s ^ link]
                low = n * rows // 2
                if len(source) == 1:
                    part = source[0][2][low : low + rows // 2]
                else:
                    part = source[n][2]
                held[s].append((s, low, to_fsdp(part, link)))
    acts_pair = [acts, to_core(acts)]
    cots_pair = [cotangent, to_core(cotangent)]

    run = functools.partial(stage, where, acts_pair, cots_pair, rows=rows)
    far = levels[-1][0]
    middle = half // 2
    halves = [(0, middle), (middle, half)]
    total = None
    for n, level in enumerate(levels[:-1]):
        entries = [x for s in level for x in held[s]]
        (total,) = run(entries, total, None, [], last=False, name=f"coords_{n}")
    coords, *far_terms = run(
        held[far], total, None, [(far, 0, rows, [], 1, halves)], last=True, name="coords_last"
    )

    landed = {s: [] for s in range(fsdp)}
    for level in reversed(levels[2:]):
        outs = far_terms
        if level != levels[-1]:
            entries = [(s, 0, rows, landed[s], 1, halves) for s in level]
            outs = run([], None, coords, entries, last=False, name="terms_far")
        outs = iter(outs)
        for s in level:
            for n, link in enumerate(links(s)):
                landed[s ^ link].append((n * middle, to_fsdp(next(outs), link)))

    grads = []
    for j in range(chunks):
        entries = [(s, j, chunk, landed[s], 1, [(0, half)]) for s in levels[1]]
        outs = run([], None, coords, entries, last=False, name=f"terms_near_{j}")
        added = [(0, to_fsdp(x, s)) for s, x in zip(levels[1], outs)]
        entries = [(0, j, chunk, added, pieces, [(0, half)])]
        outs = run([], None, coords, entries, last=False, name=f"terms_own_{j}")
        mine = outs[0]
        for k in range(1, pieces):
            mine = add_up([mine, to_piece(outs[k], k)])
        mine = add_up([mine] + [to_base(mine, k) for k in range(1, groups // pieces)])
        own_grad = [mine] + [to_piece(mine, k) for k in range(1, pieces)]
        grads.append((own_grad, [to_core(x) for x in own_grad]))

    own = [x for s in range(fsdp) for x in held[s]]
    other = [(s, low, x if s == 0 else to_core(x)) for s, low, x in own]
    proj = assemble(where, projector, own, other, rows)
    outputs = None
    for j, pair in enumerate(grads):
        for k, (mine, others) in enumerate(zip(*pair)):
            outputs = update_step(
                where, j, k, pieces, mine, others, proj, first_moment, second_moment, outputs
            )
    return tuple(outputs)


def solution(mesh):
    in_specs = (
        P(("dp", "fsdp"), None),
        P(("dp", "fsdp"), None),
        P("fsdp", None),
        P("fsdp", None),
        P("fsdp", None),
    )
    out_specs = (P("fsdp", None), P("fsdp", None), P(None, "fsdp"))
    body = functools.partial(on_device, mesh.shape["dp"], mesh.shape["fsdp"])
    return jax.shard_map(body, mesh=mesh, in_specs=in_specs, out_specs=out_specs, check_vma=False)
```

```python
import functools

import jax
import jax.numpy as jnp
from jax import lax
from jax.experimental import pallas as pl
from jax.experimental.pallas import tpu as pltpu
from jax.sharding import PartitionSpec as P

STEP = 2
CORES = 2
MIB = 1024 * 1024
BF16 = jnp.bfloat16
F32 = jnp.float32


def cost(flops, bytes_accessed):
    return pl.CostEstimate(flops=flops, bytes_accessed=bytes_accessed, transcendentals=0)


def busy(us):
    return cost(int(us * 1.15e9), 0)


def whole(array):
    zeros = (0,) * array.ndim
    return pl.BlockSpec(array.shape, lambda i, w: zeros)


def call(body, where, inputs, in_specs, out_shape, limit, scratch=(), name=None, estimate=None):
    return pl.pallas_call(
        body,
        out_shape=out_shape,
        grid_spec=pltpu.PrefetchScalarGridSpec(
            num_scalar_prefetch=1,
            grid=(1,),
            in_specs=in_specs,
            out_specs=[whole(x) for x in out_shape],
            scratch_shapes=scratch,
        ),
        compiler_params=pltpu.CompilerParams(vmem_limit_bytes=limit),
        cost_estimate=estimate,
        name=name,
    )(where, *inputs)


def cut_out(core, piece, projector, cotangent, fsdp, pieces):
    rows, rank = projector.shape
    half = rank // CORES
    tokens, width = cotangent.shape
    span = width // (fsdp * pieces)
    steps = 4

    def body(core_ref, piece_ref, proj_ref, cot_ref, proj_out, cot_out, sems):
        copies = []
        for s in range(fsdp):
            at = pl.multiple_of((s * pieces + pieces - 1 - piece_ref[0]) * span, span)
            copies.append((cot_ref.at[:, pl.ds(at, span)], cot_out.at[:, pl.ds(s * span, span)]))
        columns = pl.ds(pl.multiple_of(core_ref[0] * half, half), half)
        for n in range(steps):
            at = pl.ds(n * (rows // steps), rows // steps)
            copies.append((proj_ref.at[at, columns], proj_out.at[at, :]))
        copies = [pltpu.make_async_copy(x, y, sems.at[n]) for n, (x, y) in enumerate(copies)]
        for copy in copies:
            copy.start()
        for copy in copies:
            copy.wait()

    hbm = [pltpu.with_memory_space_constraint(x, pltpu.HBM) for x in (projector, cotangent)]
    return pl.pallas_call(
        body,
        out_shape=[
            jax.ShapeDtypeStruct((rows, half), BF16),
            jax.ShapeDtypeStruct((tokens, width // pieces), BF16),
        ],
        in_specs=[pl.BlockSpec(memory_space=pltpu.SMEM)] * 2
        + [pl.BlockSpec(memory_space=pl.ANY)] * 2,
        out_specs=[pl.BlockSpec(memory_space=pltpu.VMEM)] * 2,
        scratch_shapes=[pltpu.SemaphoreType.DMA((fsdp + steps,))],
        compiler_params=pltpu.CompilerParams(vmem_limit_bytes=8 * MIB),
        cost_estimate=busy(1),
        name="cut_out",
    )(core, piece, *hbm)


def coords_step(where, acts, proj, total, rows, last, name):
    tokens = acts[0].shape[0]
    half = proj[0][2].shape[1]
    inputs, specs = [], []
    for s, low, block in proj:
        size = block.shape[0]
        at = functools.partial(
            lambda s, low, size, i, w: (0, ((w[0] ^ s) * rows + low) // size), s, low, size
        )
        inputs += [*acts, block]
        specs += [pl.BlockSpec((tokens, size), at)] * 2 + [whole(block)]
    if total is not None:
        inputs.append(total)
        specs.append(whole(total))
    if last:
        shape = jax.ShapeDtypeStruct((half, 2 * tokens), BF16)
    else:
        shape = jax.ShapeDtypeStruct((2 * tokens, half), F32)

    def body(w, *refs):
        out = refs[len(inputs)]
        for t in range(2):
            span = slice(t * tokens, (t + 1) * tokens)
            value = None if total is None else refs[3 * len(proj)][span, :]
            for n in range(len(proj)):
                part = jnp.dot(
                    refs[3 * n + t][...], refs[3 * n + 2][...], preferred_element_type=F32
                )
                value = part if value is None else value + part
            if last:
                out[:, span] = value.T.astype(BF16)
            else:
                out[span, :] = value

    return call(
        body,
        where,
        inputs,
        specs,
        [shape],
        16 * MIB,
        name=name,
        estimate=busy(8),
    )[0]


def terms_step(where, cots, coords, span, pieces, entries, name, kind=BF16):
    tokens = cots[0][0].shape[0]
    half = coords[0].shape[0]
    inputs = list(coords)
    specs = [whole(x) for x in coords]
    out_shape = []
    for s, added, cuts in entries:
        for x, packed in cots:
            step = 1 if packed else pieces
            at = functools.partial(
                lambda s, step, i, w: (0, (w[0] ^ s) * step + (w[2] if step > 1 else 0)),
                s,
                step,
            )
            inputs.append(x)
            specs.append(pl.BlockSpec((tokens, span), at))
        for _, x in added:
            inputs.append(x)
            specs.append(whole(x))
        out_shape += [jax.ShapeDtypeStruct((b - a, span), kind) for a, b in cuts]

    def body(w, *refs):
        ins = iter(refs[len(coords) : len(inputs)])
        outs = iter(refs[len(inputs) : len(inputs) + len(out_shape)])
        value = refs[-1]
        for s, added, cuts in entries:
            term = None
            for n in range(len(cots)):
                at = slice(n % 2 * tokens, (n % 2 + 1) * tokens)
                part = jnp.dot(
                    refs[n // 2][:, at], next(ins)[...], preferred_element_type=F32
                )
                term = part if term is None else term + part
            value[...] = term
            for low, x in added:
                value[low : low + x.shape[0], :] += next(ins)[...].astype(F32)
            for a, b in cuts:
                next(outs)[...] = value[a:b, :].astype(kind)

    return call(
        body,
        where,
        inputs,
        specs,
        out_shape,
        16 * MIB,
        scratch=[pltpu.VMEM((half, span), F32)],
        name=name,
        estimate=busy(8 if kind == F32 else 1),
    )


def assemble(where, blocks, rows, parts):
    half = blocks[0][2].shape[1]
    inputs = [x for _, _, x in blocks]

    def body(w, *refs):
        out, sems = refs[-2:]
        copies = []
        for n, (s, low, x) in enumerate(blocks):
            size = x.shape[0]
            at = pl.ds(pl.multiple_of((w[0] ^ s) * rows + low, size), size)
            copies.append(pltpu.make_async_copy(refs[n], out.at[at, :], sems.at[n]))
        for copy in copies:
            copy.start()
        for copy in copies:
            copy.wait()

    return pl.pallas_call(
        body,
        out_shape=jax.ShapeDtypeStruct((parts * rows, half), BF16),
        in_specs=[pl.BlockSpec(memory_space=pltpu.SMEM)]
        + [pl.BlockSpec(memory_space=pl.ANY)] * len(inputs),
        out_specs=pl.BlockSpec(memory_space=pl.ANY),
        scratch_shapes=[pltpu.SemaphoreType.DMA((len(inputs),))],
        compiler_params=pltpu.CompilerParams(vmem_limit_bytes=4 * MIB),
        cost_estimate=busy(2),
        name="assemble",
    )(where, *inputs)


def update_step(where, k, pieces, own_grad, other_grad, own_proj, other_proj, moments, before):
    half, span = own_grad.shape
    rank = CORES * half
    features = moments[0].shape[0]
    width = own_proj.shape[0]
    rows = min(1024, width)
    steps = width // rows
    part = min(256, rows)

    def body(w, *refs):
        grads, projs, ins = refs[:2], refs[2:4], refs[4:6]
        first_out, second_out, update = refs[-11:-8]
        moment, proj, direction, out = refs[-8:-4]
        moment_in, moment_out, proj_in, update_out = refs[-4:]
        base = lax.rem(w[2] + pieces - k, pieces) * span
        features_at = pl.ds(pl.multiple_of(base, span), span)

        def columns(h):
            core = w[1] if h == 0 else 1 - w[1]
            return pl.ds(pl.multiple_of(core * half, half), half)

        def here(h):
            return pl.ds(h * half, half)

        loads = [
            [
                pltpu.make_async_copy(
                    ins[n].at[features_at, columns(h)],
                    moment.at[n, :, here(h)],
                    moment_in.at[h, n],
                )
                for n in range(2)
            ]
            for h in range(2)
        ]
        stores = [
            [
                pltpu.make_async_copy(
                    moment.at[n, :, here(h)],
                    (first_out, second_out)[n].at[features_at, columns(h)],
                    moment_out.at[h, n],
                )
                for n in range(2)
            ]
            for h in range(2)
        ]
        proj_loads = [
            [
                pltpu.make_async_copy(
                    projs[h].at[pl.ds(r * rows, rows), :],
                    proj.at[pl.ds(r * rows, rows), here(h)],
                    proj_in.at[h, r],
                )
                for h in range(2)
            ]
            for r in range(steps)
        ]
        update_stores = [
            [
                pltpu.make_async_copy(
                    out.at[pl.ds(r * rows + m * part, part), :],
                    update.at[pl.ds(r * rows + m * part, part), features_at],
                    update_out.at[r, m],
                )
                for m in range(rows // part)
            ]
            for r in range(steps)
        ]
        for copy in sum(loads, []) + sum(proj_loads, []):
            copy.start()
        first_scale = 1.0 / (1.0 - 0.9**STEP)
        second_scale = 1.0 / (1.0 - 0.999**STEP)
        for h in range(2):
            grad_low = grads[h][...].T.astype(F32)
            for copy in loads[h]:
                copy.wait()
            first_new = 0.9 * moment[0, :, here(h)] + 0.1 * grad_low
            second_new = 0.999 * moment[1, :, here(h)] + 0.001 * grad_low * grad_low
            moment[0, :, here(h)] = first_new
            moment[1, :, here(h)] = second_new
            for copy in stores[h]:
                copy.start()
            ratio = (first_new * first_scale) / (jnp.sqrt(second_new * second_scale) + 1e-08)
            direction[here(h), :] = ratio.astype(BF16).T
        for r in range(steps):
            for copy in proj_loads[r]:
                copy.wait()
            at = pl.ds(r * rows, rows)
            out[at, :] = jnp.dot(proj[at, :], direction[...], preferred_element_type=F32)
            for copy in update_stores[r]:
                copy.start()
        for copy in sum(stores, []) + sum(update_stores, []):
            copy.wait()

    inputs = [own_grad, other_grad, own_proj, other_proj, *moments]
    any_space = pl.BlockSpec(memory_space=pl.ANY)
    in_specs = [whole(own_grad), whole(other_grad)] + [any_space] * 4
    aliases = {}
    if before is not None:
        aliases = {1 + len(inputs) + n: n for n in range(3)}
        inputs += before
        in_specs += [any_space] * 3
    return pl.pallas_call(
        body,
        out_shape=[jax.ShapeDtypeStruct(x.shape, F32) for x in moments]
        + [jax.ShapeDtypeStruct((width, features), F32)],
        grid_spec=pltpu.PrefetchScalarGridSpec(
            num_scalar_prefetch=1,
            grid=(1,),
            in_specs=in_specs,
            out_specs=[any_space] * 3,
            scratch_shapes=[
                pltpu.VMEM((2, span, rank), F32),
                pltpu.VMEM((width, rank), BF16),
                pltpu.VMEM((rank, span), BF16),
                pltpu.VMEM((width, span), F32),
                pltpu.SemaphoreType.DMA((2, 2)),
                pltpu.SemaphoreType.DMA((2, 2)),
                pltpu.SemaphoreType.DMA((2, steps)),
                pltpu.SemaphoreType.DMA((steps, rows // part)),
            ],
        ),
        input_output_aliases=aliases,
        compiler_params=pltpu.CompilerParams(vmem_limit_bytes=28 * MIB),
        cost_estimate=cost(2 * width * rank * span, 4 * width * span + 18 * span * rank),
        name="update_step",
    )(where, *inputs)


def after(x, *others):
    return lax.optimization_barrier((x, *others))[0]


def add_up(arrays):
    return functools.reduce(jnp.add, [x.astype(F32) for x in arrays]).astype(BF16)


def on_device(dp, fsdp, acts, cotangent, projector, first_moment, second_moment):
    rows, rank = projector.shape
    half = rank // CORES
    groups = dp // CORES
    pieces = 2 if groups % 2 == 0 else 1
    span = rows // pieces
    fsdp_at = lax.axis_index("fsdp")
    dp_at = lax.axis_index("dp")
    where = jnp.stack([fsdp_at, dp_at % CORES, (dp_at // CORES) % pieces]).astype(jnp.int32)

    def to_core(x):
        return lax.ppermute(x, "dp", [(i, i ^ 1) for i in range(dp)])

    def to_fsdp(x, s):
        return lax.ppermute(x, "fsdp", [(i, i ^ s) for i in range(fsdp)])

    def to_piece(x, k):
        pairs = []
        for i in range(dp):
            group, core = divmod(i, CORES)
            base = group - group % pieces
            pairs.append((i, (base + (group + k) % pieces) * CORES + core))
        return lax.ppermute(x, "dp", pairs)

    def to_base(x, k):
        return lax.ppermute(x, "dp", [(i, (i + k * pieces * CORES) % dp) for i in range(dp)])

    def links(s):
        return (s & -s, 1 << (s.bit_length() - 1))

    levels = [
        [s for s in range(fsdp) if s.bit_count() == n] for n in range(fsdp.bit_length())
    ]

    part = rows // 2
    piece_at = ((dp_at // CORES) % pieces).astype(jnp.int32)
    core_at = (dp_at % CORES).astype(jnp.int32)
    own_half, cot_out = cut_out(
        core_at[None], piece_at[None], projector, cotangent, fsdp, pieces
    )
    held = {0: [(0, 0, own_half)]}
    for level in levels[1:]:
        for s in level:
            if s.bit_count() == 1:
                held[s] = [(s, 0, to_fsdp(own_half, s))]
                continue
            held[s] = []
            for n, link in enumerate(links(s)):
                source = held[s ^ link]
                x = source[n][2] if len(source) > 1 else source[0][2][n * part : (n + 1) * part]
                held[s].append((s, n * part, to_fsdp(x, link)))
    acts_pair = [acts, to_core(acts)]
    cots = [(cotangent, False), (to_core(after(cotangent, own_half)), False)]

    total = None
    for n, level in enumerate(levels):
        entries = [x for s in level for x in held[s]]
        last = n == len(levels) - 1
        total = coords_step(where, acts_pair, entries, total, rows, last, f"coords_{n}")
    coords = [total]
    landed = {s: [] for s in range(fsdp)}
    if pieces > 1:
        coords = [to_piece(total, 1)]
        entries = [(s, [], [(0, half)]) for s in range(fsdp)]
        sums = terms_step(where, cots, [total], span, pieces, entries, "terms_chip", F32)
        for s in range(fsdp):
            landed[s].append((0, sums[s]))
        arrived = after(to_piece(cot_out, 1), *sums)
        cots = [(arrived, True), (to_core(arrived), True)]

    middle = half // 2
    halves = [(0, middle), (middle, half)]
    for n in range(len(levels) - 1, -1, -1):
        level = levels[n]
        cuts = halves if n > 1 else [(0, half)]
        entries = [(s, landed[s], cuts) for s in level]
        outs = terms_step(where, cots, coords, span, pieces, entries, f"terms_{n}")
        outs = iter(outs)
        for s in level:
            if n > 1:
                for m, link in enumerate(links(s)):
                    landed[s ^ link].append((m * middle, to_fsdp(next(outs), link)))
            elif n == 1:
                landed[0].append((0, to_fsdp(next(outs), s)))
            else:
                mine = next(outs)
    mine = add_up([mine] + [to_base(mine, k) for k in range(1, groups // pieces)])
    grads = [mine] + [to_piece(mine, k) for k in range(1, pieces)]

    blocks = [(s, low, after(x, *coords)) for s in range(fsdp) for s, low, x in held[s]]
    own_proj = assemble(where, blocks, rows, fsdp)
    other_proj = to_core(own_proj)
    outputs = None
    for k, grad in enumerate(grads):
        if outputs is not None:
            grad = after(grad, *outputs)
        outputs = update_step(
            where,
            k,
            pieces,
            grad,
            to_core(grad),
            own_proj,
            other_proj,
            (first_moment, second_moment),
            outputs,
        )
    return tuple(outputs)


def solution(mesh):
    in_specs = (
        P(("dp", "fsdp"), None),
        P(("dp", "fsdp"), None),
        P("fsdp", None),
        P("fsdp", None),
        P("fsdp", None),
    )
    out_specs = (P("fsdp", None), P("fsdp", None), P(None, "fsdp"))
    body = functools.partial(on_device, mesh.shape["dp"], mesh.shape["fsdp"])
    return jax.shard_map(body, mesh=mesh, in_specs=in_specs, out_specs=out_specs, check_vma=False)
```

```python
import functools

import jax
import jax.numpy as jnp
from jax import lax
from jax.experimental import pallas as pl
from jax.experimental.pallas import tpu as pltpu
from jax.sharding import PartitionSpec as P

STEP = 2
CORES = 2
MIB = 1024 * 1024
BF16 = jnp.bfloat16
F32 = jnp.float32


def cost(flops, bytes_accessed):
    return pl.CostEstimate(flops=flops, bytes_accessed=bytes_accessed, transcendentals=0)


def busy(us):
    return cost(int(us * 1.15e9), 0)


def whole(array):
    zeros = (0,) * array.ndim
    return pl.BlockSpec(array.shape, lambda i, w: zeros)


def call(body, where, inputs, in_specs, out_shape, limit, scratch=(), name=None, estimate=None):
    return pl.pallas_call(
        body,
        out_shape=out_shape,
        grid_spec=pltpu.PrefetchScalarGridSpec(
            num_scalar_prefetch=1,
            grid=(1,),
            in_specs=in_specs,
            out_specs=[whole(x) for x in out_shape],
            scratch_shapes=scratch,
        ),
        compiler_params=pltpu.CompilerParams(vmem_limit_bytes=limit),
        cost_estimate=estimate,
        name=name,
    )(where, *inputs)


def cut_out(fsdp_at, core, piece, projector, cotangent, fsdp, pieces):
    rows, rank = projector.shape
    half = rank // CORES
    tokens, width = cotangent.shape
    span = width // (fsdp * pieces)
    steps = 4

    def body(fsdp_ref, core_ref, piece_ref, proj_ref, cot_ref, proj_out, cot_out, sems):
        copies = []
        for s in range(1, fsdp):
            block = (fsdp_ref[0] ^ s) * pieces + pieces - 1 - piece_ref[0]
            source = cot_ref.at[:, pl.ds(pl.multiple_of(block * span, span), span)]
            copies.append((source, cot_out.at[:, pl.ds((s - 1) * span, span)]))
        columns = pl.ds(pl.multiple_of(core_ref[0] * half, half), half)
        for n in range(steps):
            at = pl.ds(n * (rows // steps), rows // steps)
            copies.append((proj_ref.at[at, columns], proj_out.at[at, :]))
        copies = [pltpu.make_async_copy(x, y, sems.at[n]) for n, (x, y) in enumerate(copies)]
        for copy in copies:
            copy.start()
        for copy in copies:
            copy.wait()

    hbm = [pltpu.with_memory_space_constraint(x, pltpu.HBM) for x in (projector, cotangent)]
    return pl.pallas_call(
        body,
        out_shape=[
            jax.ShapeDtypeStruct((rows, half), BF16),
            jax.ShapeDtypeStruct((tokens, (fsdp - 1) * span), BF16),
        ],
        in_specs=[pl.BlockSpec(memory_space=pltpu.SMEM)] * 3
        + [pl.BlockSpec(memory_space=pl.ANY)] * 2,
        out_specs=[pl.BlockSpec(memory_space=pltpu.VMEM)] * 2,
        scratch_shapes=[pltpu.SemaphoreType.DMA((fsdp + steps,))],
        compiler_params=pltpu.CompilerParams(vmem_limit_bytes=8 * MIB),
        cost_estimate=busy(1),
        name="cut_out",
    )(fsdp_at, core, piece, *hbm)


def coords_step(where, acts, proj, total, rows, last, name):
    tokens = acts[0].shape[0]
    half = proj[0][2].shape[1]
    inputs, specs = [], []
    for s, low, block in proj:
        size = block.shape[0]
        at = functools.partial(
            lambda s, low, size, i, w: (0, ((w[0] ^ s) * rows + low) // size), s, low, size
        )
        inputs += [*acts, block]
        specs += [pl.BlockSpec((tokens, size), at)] * 2 + [whole(block)]
    if total is not None:
        inputs.append(total)
        specs.append(whole(total))
    if last:
        shape = jax.ShapeDtypeStruct((half, 2 * tokens), BF16)
    else:
        shape = jax.ShapeDtypeStruct((2 * tokens, half), F32)

    def body(w, *refs):
        out = refs[len(inputs)]
        for t in range(2):
            span = slice(t * tokens, (t + 1) * tokens)
            value = None if total is None else refs[3 * len(proj)][span, :]
            for n in range(len(proj)):
                part = jnp.dot(
                    refs[3 * n + t][...], refs[3 * n + 2][...], preferred_element_type=F32
                )
                value = part if value is None else value + part
            if last:
                out[:, span] = value.T.astype(BF16)
            else:
                out[span, :] = value

    return call(
        body,
        where,
        inputs,
        specs,
        [shape],
        16 * MIB,
        name=name,
        estimate=busy(8),
    )[0]


def terms_step(where, cots, coords, entries, pieces, span, chunk, name, kind=BF16, estimate=1):
    per_piece = span // chunk
    half = entries[0][4][-1][1]
    inputs = [] if coords is None else [coords]
    specs = [whole(x) for x in inputs]
    out_shape = []
    for s, other, j, added, cuts in entries:
        for x, packed in cots:
            if packed and s == 0:
                continue

            def at(i, w, s=s, other=other, j=j, packed=packed):
                if packed:
                    return (0, (s - 1) * per_piece + j)
                piece = lax.rem(w[2] + other, pieces)
                return (0, ((w[0] ^ s) * pieces + piece) * per_piece + j)

            inputs.append(x)
            specs.append(pl.BlockSpec((x.shape[0], chunk), at))
        for _, x in added:
            column = j if x.shape[1] > chunk else 0
            at = functools.partial(lambda c, i, w: (0, c), column)
            inputs.append(x)
            specs.append(pl.BlockSpec((x.shape[0], chunk), at))
        out_shape += [jax.ShapeDtypeStruct((b - a, chunk), kind) for a, b in cuts]

    def body(w, *refs):
        ins = iter(refs[: len(inputs)])
        outs = iter(refs[len(inputs) : len(inputs) + len(out_shape)])
        value = refs[-1]
        coords_ref = None if coords is None else next(ins)
        for s, _, _, added, cuts in entries:
            term = None
            for n, (x, packed) in enumerate(cots):
                if packed and s == 0:
                    continue
                tokens = x.shape[0]
                part = jnp.dot(
                    coords_ref[:, n * tokens : (n + 1) * tokens],
                    next(ins)[...],
                    preferred_element_type=F32,
                )
                term = part if term is None else term + part
            extra = [(low, x.shape[0], next(ins)) for low, x in added]
            for low, size, ref in extra:
                if size == half:
                    part = ref[...].astype(F32)
                    term = part if term is None else term + part
            value[...] = term
            for low, size, ref in extra:
                if size < half:
                    value[low : low + size, :] += ref[...].astype(F32)
            for a, b in cuts:
                next(outs)[...] = value[a:b, :].astype(kind)

    return call(
        body,
        where,
        inputs,
        specs,
        out_shape,
        20 * MIB,
        scratch=[pltpu.VMEM((half, chunk), F32)],
        name=name,
        estimate=busy(estimate),
    )


def assemble(where, blocks, rows, parts):
    half = blocks[0][2].shape[1]
    inputs = [x for _, _, x in blocks]

    def body(w, *refs):
        out, sems = refs[-2:]
        copies = []
        for n, (s, low, x) in enumerate(blocks):
            size = x.shape[0]
            at = pl.ds(pl.multiple_of((w[0] ^ s) * rows + low, size), size)
            copies.append(pltpu.make_async_copy(refs[n], out.at[at, :], sems.at[n]))
        for copy in copies:
            copy.start()
        for copy in copies:
            copy.wait()

    return pl.pallas_call(
        body,
        out_shape=jax.ShapeDtypeStruct((parts * rows, half), BF16),
        in_specs=[pl.BlockSpec(memory_space=pltpu.SMEM)]
        + [pl.BlockSpec(memory_space=pl.ANY)] * len(inputs),
        out_specs=pl.BlockSpec(memory_space=pl.ANY),
        scratch_shapes=[pltpu.SemaphoreType.DMA((len(inputs),))],
        compiler_params=pltpu.CompilerParams(vmem_limit_bytes=4 * MIB),
        cost_estimate=busy(2),
        name="assemble",
    )(where, *inputs)


def update_step(where, k, pieces, low, grads, own_proj, other_proj, moments, before):
    half, chunk = grads[0][0].shape
    span = chunk * len(grads)
    rank = CORES * half
    features = moments[0].shape[0]
    width = own_proj.shape[0]
    rows = min(1024, width)
    steps = width // rows
    part = min(256, rows)
    flat = [x for pair in grads for x in pair]

    def body(w, *refs):
        grad_refs, refs = refs[: len(flat)], refs[len(flat) :]
        projs, ins = refs[:2], refs[2:4]
        first_out, second_out, update = refs[-11:-8]
        moment, proj, direction, out = refs[-8:-4]
        moment_in, moment_out, proj_in, update_out = refs[-4:]
        base = lax.rem(w[2] + pieces - k, pieces) * (features // pieces) + low
        features_at = pl.ds(pl.multiple_of(base, chunk), span)

        def columns(h):
            core = w[1] if h == 0 else 1 - w[1]
            return pl.ds(pl.multiple_of(core * half, half), half)

        def here(h):
            return pl.ds(h * half, half)

        def each(make):
            return [[make(h, n) for n in range(2)] for h in range(2)]

        loads = each(
            lambda h, n: pltpu.make_async_copy(
                ins[n].at[features_at, columns(h)], moment.at[n, :, here(h)], moment_in.at[h, n]
            )
        )
        stores = each(
            lambda h, n: pltpu.make_async_copy(
                moment.at[n, :, here(h)],
                (first_out, second_out)[n].at[features_at, columns(h)],
                moment_out.at[h, n],
            )
        )
        proj_loads = [
            [
                pltpu.make_async_copy(
                    projs[h].at[pl.ds(r * rows, rows), :],
                    proj.at[pl.ds(r * rows, rows), here(h)],
                    proj_in.at[h, r],
                )
                for h in range(2)
            ]
            for r in range(steps)
        ]
        update_stores = [
            [
                pltpu.make_async_copy(
                    out.at[pl.ds(r * rows + m * part, part), :],
                    update.at[pl.ds(r * rows + m * part, part), features_at],
                    update_out.at[r, m],
                )
                for m in range(rows // part)
            ]
            for r in range(steps)
        ]
        for copy in sum(loads, []) + sum(proj_loads, []):
            copy.start()
        first_scale = 1.0 / (1.0 - 0.9**STEP)
        second_scale = 1.0 / (1.0 - 0.999**STEP)
        for h in range(2):
            for copy in loads[h]:
                copy.wait()
            for m in range(len(grads)):
                at = pl.ds(m * chunk, chunk)
                grad_low = grad_refs[2 * m + h][...].T.astype(F32)
                first_new = 0.9 * moment[0, at, here(h)] + 0.1 * grad_low
                second_new = 0.999 * moment[1, at, here(h)] + 0.001 * grad_low * grad_low
                moment[0, at, here(h)] = first_new
                moment[1, at, here(h)] = second_new
                ratio = (first_new * first_scale) / (
                    jnp.sqrt(second_new * second_scale) + 1e-08
                )
                direction[here(h), at] = ratio.astype(BF16).T
            for copy in stores[h]:
                copy.start()
        for r in range(steps):
            for copy in proj_loads[r]:
                copy.wait()
            at = pl.ds(r * rows, rows)
            out[at, :] = jnp.dot(proj[at, :], direction[...], preferred_element_type=F32)
            for copy in update_stores[r]:
                copy.start()
        for copy in sum(stores, []) + sum(update_stores, []):
            copy.wait()

    inputs = [*flat, own_proj, other_proj, *moments]
    any_space = pl.BlockSpec(memory_space=pl.ANY)
    in_specs = [whole(x) for x in flat] + [any_space] * 4
    aliases = {}
    if before is not None:
        aliases = {1 + len(inputs) + n: n for n in range(3)}
        inputs += before
        in_specs += [any_space] * 3
    return pl.pallas_call(
        body,
        out_shape=[jax.ShapeDtypeStruct(x.shape, F32) for x in moments]
        + [jax.ShapeDtypeStruct((width, features), F32)],
        grid_spec=pltpu.PrefetchScalarGridSpec(
            num_scalar_prefetch=1,
            grid=(1,),
            in_specs=in_specs,
            out_specs=[any_space] * 3,
            scratch_shapes=[
                pltpu.VMEM((2, span, rank), F32),
                pltpu.VMEM((width, rank), BF16),
                pltpu.VMEM((rank, span), BF16),
                pltpu.VMEM((width, span), F32),
                pltpu.SemaphoreType.DMA((2, 2)),
                pltpu.SemaphoreType.DMA((2, 2)),
                pltpu.SemaphoreType.DMA((2, steps)),
                pltpu.SemaphoreType.DMA((steps, rows // part)),
            ],
        ),
        input_output_aliases=aliases,
        compiler_params=pltpu.CompilerParams(vmem_limit_bytes=28 * MIB),
        cost_estimate=busy(6),
        name="update_step",
    )(where, *inputs)


def in_vmem(x):
    return pltpu.with_memory_space_constraint(x, pltpu.VMEM)


def after(x, *others):
    return lax.optimization_barrier((x, *others))[0]


def add_up(arrays):
    return functools.reduce(jnp.add, [x.astype(F32) for x in arrays]).astype(BF16)


def on_device(dp, fsdp, acts, cotangent, projector, first_moment, second_moment):
    rows, rank = projector.shape
    half = rank // CORES
    groups = dp // CORES
    pieces = 2 if groups % 2 == 0 else 1
    span = rows // pieces
    chunk = span // 2 if span % 256 == 0 else span
    chunks = range(span // chunk)
    fsdp_at = lax.axis_index("fsdp").astype(jnp.int32)
    dp_at = lax.axis_index("dp")
    core_at = (dp_at % CORES).astype(jnp.int32)
    piece_at = ((dp_at // CORES) % pieces).astype(jnp.int32)
    where = jnp.stack([fsdp_at, core_at, piece_at])

    def to_core(x):
        return lax.ppermute(x, "dp", [(i, i ^ 1) for i in range(dp)])

    def to_fsdp(x, s):
        return lax.ppermute(x, "fsdp", [(i, i ^ s) for i in range(fsdp)])

    def to_piece(x, k):
        pairs = []
        for i in range(dp):
            group, core = divmod(i, CORES)
            base = group - group % pieces
            pairs.append((i, (base + (group + k) % pieces) * CORES + core))
        return lax.ppermute(x, "dp", pairs)

    def to_base(x, k):
        return lax.ppermute(x, "dp", [(i, (i + k * pieces * CORES) % dp) for i in range(dp)])

    def links(s):
        return (s & -s, 1 << (s.bit_length() - 1))

    levels = [
        [s for s in range(fsdp) if s.bit_count() == n] for n in range(fsdp.bit_length())
    ]

    part = rows // 2
    own_half, cot_out = cut_out(
        fsdp_at[None], core_at[None], piece_at[None], projector, cotangent, fsdp, pieces
    )
    held = {0: [(0, 0, own_half)]}
    for level in levels[1:]:
        for s in level:
            if s.bit_count() == 1:
                held[s] = [(s, 0, to_fsdp(own_half, s))]
                continue
            held[s] = []
            for n, link in enumerate(links(s)):
                source = held[s ^ link]
                x = source[n][2] if len(source) > 1 else source[0][2][n * part : (n + 1) * part]
                held[s].append((s, n * part, to_fsdp(x, link)))
    acts_pair = [acts, in_vmem(to_core(acts))]
    cots = [(cotangent, False), (in_vmem(to_core(after(cotangent, own_half))), False)]

    total = None
    for n, level in enumerate(levels):
        entries = [x for s in level for x in held[s]]
        last = n == len(levels) - 1
        total = coords_step(where, acts_pair, entries, total, rows, last, f"coords_{n}")
    full = [(0, half)]
    entries = [(s, 0, 0, [], full) for s in range(fsdp)]
    far_coords = None
    if pieces > 1:
        far_coords = to_piece(total, 1)
    sums = terms_step(
        where, cots, total, entries, pieces, span, span, "terms_chip", F32, 12
    )
    landed = {s: [(0, x)] for s, x in enumerate(sums)}
    cots_far = []
    if pieces > 1:
        arrived = after(to_piece(cot_out, 1), total)
        cots_far = [(arrived, True), (in_vmem(to_core(arrived)), True)]
        entries = [(0, 1, 0, [], full)]
        (pair_sum,) = terms_step(
            where, cots, total, entries, pieces, span, span, "terms_pair"
        )
        landed[0].append((0, to_piece(pair_sum, 1)))

    middle = half // 2
    halves = [(0, middle), (middle, half)]
    for n in range(len(levels) - 1, 1, -1):
        entries = [(s, 0, 0, landed[s], halves) for s in levels[n]]
        outs = iter(
            terms_step(
                where, cots_far, far_coords, entries, pieces, span, span, f"terms_{n}"
            )
        )
        for s in levels[n]:
            for m, link in enumerate(links(s)):
                landed[s ^ link].append((m * middle, to_fsdp(next(outs), link)))
    near = {j: [] for j in chunks}
    if fsdp > 1:
        entries = [(s, 0, j, landed[s], full) for j in chunks for s in levels[1]]
        outs = terms_step(
            where, cots_far, far_coords, entries, pieces, span, chunk, "terms_1"
        )
        for (s, _, j, _, _), x in zip(entries, outs):
            near[j].append((0, to_fsdp(x, s)))
    parts = []
    for j in chunks:
        entries = [(0, 0, j, landed[0] + near[j], full)]
        (x,) = terms_step(where, [], None, entries, pieces, span, chunk, "terms_0", BF16, 1)
        parts.append([x] + [to_base(x, k) for k in range(1, groups // pieces)])
    parts[0] = [after(x, parts[-1][0]) for x in parts[0]]

    blocks = [(s, low, after(x, total)) for s in range(fsdp) for s, low, x in held[s]]
    own_proj = assemble(where, blocks, rows, fsdp)
    other_proj = to_core(own_proj)
    common = (own_proj, other_proj, (first_moment, second_moment))
    outputs, others = None, []
    for j in chunks:
        if outputs is not None:
            parts[j] = [after(x, *outputs, *others) for x in parts[j]]
        mine = add_up(parts[j])
        if pieces > 1:
            others.append(to_piece(mine, 1))
        pair = (mine, to_core(mine))
        outputs = update_step(where, 0, pieces, j * chunk, [pair], *common, outputs)
    if pieces > 1:
        pairs = [(x, to_core(after(x, *outputs))) for x in others]
        outputs = update_step(where, 1, pieces, 0, pairs, *common, outputs)
    return tuple(outputs)


def solution(mesh):
    in_specs = (
        P(("dp", "fsdp"), None),
        P(("dp", "fsdp"), None),
        P("fsdp", None),
        P("fsdp", None),
        P("fsdp", None),
    )
    out_specs = (P("fsdp", None), P("fsdp", None), P(None, "fsdp"))
    body = functools.partial(on_device, mesh.shape["dp"], mesh.shape["fsdp"])
    return jax.shard_map(body, mesh=mesh, in_specs=in_specs, out_specs=out_specs, check_vma=False)
```

```python
import functools

import jax
import jax.numpy as jnp
from jax import lax
from jax.experimental import pallas as pl
from jax.experimental.pallas import tpu as pltpu
from jax.sharding import PartitionSpec as P

STEP = 2
CORES = 2
MIB = 1024 * 1024
BF16 = jnp.bfloat16
F32 = jnp.float32


def cost(flops, bytes_accessed):
    return pl.CostEstimate(flops=flops, bytes_accessed=bytes_accessed, transcendentals=0)


def busy(us):
    return cost(int(us * 1.15e9), 0)


def whole(array):
    zeros = (0,) * array.ndim
    return pl.BlockSpec(array.shape, lambda i, w: zeros)


def call(body, where, inputs, in_specs, out_shape, limit, scratch=(), name=None, estimate=None):
    return pl.pallas_call(
        body,
        out_shape=out_shape,
        grid_spec=pltpu.PrefetchScalarGridSpec(
            num_scalar_prefetch=1,
            grid=(1,),
            in_specs=in_specs,
            out_specs=[whole(x) for x in out_shape],
            scratch_shapes=scratch,
        ),
        compiler_params=pltpu.CompilerParams(vmem_limit_bytes=limit),
        cost_estimate=estimate,
        name=name,
    )(where, *inputs)


def cut_out(fsdp_at, core, piece, projector, cotangent, fsdp, pieces):
    rows, rank = projector.shape
    half = rank // CORES
    tokens, width = cotangent.shape
    span = width // (fsdp * pieces)
    steps = 4

    def body(fsdp_ref, core_ref, piece_ref, proj_ref, cot_ref, proj_out, cot_out, sems):
        copies = []
        for s in range(1, fsdp):
            block = (fsdp_ref[0] ^ s) * pieces + pieces - 1 - piece_ref[0]
            source = cot_ref.at[:, pl.ds(pl.multiple_of(block * span, span), span)]
            copies.append((source, cot_out.at[:, pl.ds((s - 1) * span, span)]))
        columns = pl.ds(pl.multiple_of(core_ref[0] * half, half), half)
        for n in range(steps):
            at = pl.ds(n * (rows // steps), rows // steps)
            copies.append((proj_ref.at[at, columns], proj_out.at[at, :]))
        copies = [pltpu.make_async_copy(x, y, sems.at[n]) for n, (x, y) in enumerate(copies)]
        for copy in copies:
            copy.start()
        for copy in copies:
            copy.wait()

    hbm = [pltpu.with_memory_space_constraint(x, pltpu.HBM) for x in (projector, cotangent)]
    return pl.pallas_call(
        body,
        out_shape=[
            jax.ShapeDtypeStruct((rows, half), BF16),
            jax.ShapeDtypeStruct((tokens, (fsdp - 1) * span), BF16),
        ],
        in_specs=[pl.BlockSpec(memory_space=pltpu.SMEM)] * 3
        + [pl.BlockSpec(memory_space=pl.ANY)] * 2,
        out_specs=[pl.BlockSpec(memory_space=pltpu.VMEM)] * 2,
        scratch_shapes=[pltpu.SemaphoreType.DMA((fsdp + steps,))],
        compiler_params=pltpu.CompilerParams(vmem_limit_bytes=8 * MIB),
        cost_estimate=busy(1),
        name="cut_out",
    )(fsdp_at, core, piece, *hbm)


def coords_step(where, acts, proj, total, rows, last, name):
    tokens = acts[0].shape[0]
    half = proj[0][2].shape[1]
    inputs, specs = [], []
    for s, low, block in proj:
        size = block.shape[0]
        at = functools.partial(
            lambda s, low, size, i, w: (0, ((w[0] ^ s) * rows + low) // size), s, low, size
        )
        inputs += [*acts, block]
        specs += [pl.BlockSpec((tokens, size), at)] * 2 + [whole(block)]
    if total is not None:
        inputs.append(total)
        specs.append(whole(total))
    if last:
        shape = jax.ShapeDtypeStruct((half, 2 * tokens), BF16)
    else:
        shape = jax.ShapeDtypeStruct((2 * tokens, half), F32)

    def body(w, *refs):
        out = refs[len(inputs)]
        for t in range(2):
            span = slice(t * tokens, (t + 1) * tokens)
            value = None if total is None else refs[3 * len(proj)][span, :]
            for n in range(len(proj)):
                part = jnp.dot(
                    refs[3 * n + t][...], refs[3 * n + 2][...], preferred_element_type=F32
                )
                value = part if value is None else value + part
            if last:
                out[:, span] = value.T.astype(BF16)
            else:
                out[span, :] = value

    return call(
        body,
        where,
        inputs,
        specs,
        [shape],
        16 * MIB,
        name=name,
        estimate=busy(8),
    )[0]


def terms_step(where, cots, coords, entries, pieces, span, chunk, name, kind=BF16, estimate=1):
    per_piece = span // chunk
    half = entries[0][4][-1][1]
    inputs = [] if coords is None else [coords]
    specs = [whole(x) for x in inputs]
    out_shape = []
    for s, other, j, added, cuts in entries:
        for x, packed in cots:
            if packed and s == 0:
                continue

            def at(i, w, s=s, other=other, j=j, packed=packed):
                if packed:
                    return (0, (s - 1) * per_piece + j)
                piece = lax.rem(w[2] + other, pieces)
                return (0, ((w[0] ^ s) * pieces + piece) * per_piece + j)

            inputs.append(x)
            specs.append(pl.BlockSpec((x.shape[0], chunk), at))
        for _, x in added:
            column = j if x.shape[1] > chunk else 0
            at = functools.partial(lambda c, i, w: (0, c), column)
            inputs.append(x)
            specs.append(pl.BlockSpec((x.shape[0], chunk), at))
        out_shape += [jax.ShapeDtypeStruct((b - a, chunk), kind) for a, b in cuts]

    def body(w, *refs):
        ins = iter(refs[: len(inputs)])
        outs = iter(refs[len(inputs) : len(inputs) + len(out_shape)])
        value = refs[-1]
        coords_ref = None if coords is None else next(ins)
        for s, _, _, added, cuts in entries:
            term = None
            for n, (x, packed) in enumerate(cots):
                if packed and s == 0:
                    continue
                tokens = x.shape[0]
                part = jnp.dot(
                    coords_ref[:, n * tokens : (n + 1) * tokens],
                    next(ins)[...],
                    preferred_element_type=F32,
                )
                term = part if term is None else term + part
            extra = [(low, x.shape[0], next(ins)) for low, x in added]
            for low, size, ref in extra:
                if size == half:
                    part = ref[...].astype(F32)
                    term = part if term is None else term + part
            value[...] = term
            for low, size, ref in extra:
                if size < half:
                    value[low : low + size, :] += ref[...].astype(F32)
            for a, b in cuts:
                next(outs)[...] = value[a:b, :].astype(kind)

    return call(
        body,
        where,
        inputs,
        specs,
        out_shape,
        20 * MIB,
        scratch=[pltpu.VMEM((half, chunk), F32)],
        name=name,
        estimate=busy(estimate),
    )


def assemble(where, blocks, rows, parts):
    half = blocks[0][2].shape[1]
    inputs = [x for _, _, x in blocks]

    def body(w, *refs):
        out, sems = refs[-2:]
        copies = []
        for n, (s, low, x) in enumerate(blocks):
            size = x.shape[0]
            at = pl.ds(pl.multiple_of((w[0] ^ s) * rows + low, size), size)
            copies.append(pltpu.make_async_copy(refs[n], out.at[at, :], sems.at[n]))
        for copy in copies:
            copy.start()
        for copy in copies:
            copy.wait()

    return pl.pallas_call(
        body,
        out_shape=jax.ShapeDtypeStruct((parts * rows, half), BF16),
        in_specs=[pl.BlockSpec(memory_space=pltpu.SMEM)]
        + [pl.BlockSpec(memory_space=pl.ANY)] * len(inputs),
        out_specs=pl.BlockSpec(memory_space=pl.ANY),
        scratch_shapes=[pltpu.SemaphoreType.DMA((len(inputs),))],
        compiler_params=pltpu.CompilerParams(vmem_limit_bytes=4 * MIB),
        cost_estimate=busy(2),
        name="assemble",
    )(where, *inputs)


def update_step(where, k, pieces, low, grads, own_proj, other_proj, moments, before):
    half, chunk = grads[0][0].shape
    span = chunk * len(grads)
    rank = CORES * half
    features = moments[0].shape[0]
    width = own_proj.shape[0]
    rows = min(1024, width)
    steps = width // rows
    part = min(256, rows)
    flat = [x for pair in grads for x in pair]

    def body(w, *refs):
        grad_refs, refs = refs[: len(flat)], refs[len(flat) :]
        own, other, ins = refs[0], refs[1], refs[2:4]
        outs, update = refs[-9:-7], refs[-7]
        moment, direction, out = refs[-6:-3]
        moment_in, moment_out, update_out = refs[-3:]
        base = lax.rem(w[2] + pieces - k, pieces) * (features // pieces) + low
        features_at = pl.ds(pl.multiple_of(base, chunk), span)
        own_rows = pl.ds(pl.multiple_of(w[1] * half, half), half)
        other_rows = pl.ds(pl.multiple_of((1 - w[1]) * half, half), half)
        loads = [
            pltpu.make_async_copy(ins[n].at[features_at, :], moment.at[n], moment_in.at[n])
            for n in range(2)
        ]
        stores = [
            pltpu.make_async_copy(moment.at[n], outs[n].at[features_at, :], moment_out.at[n])
            for n in range(2)
        ]
        update_stores = [
            [
                pltpu.make_async_copy(
                    out.at[pl.ds(r * rows + m * part, part), :],
                    update.at[pl.ds(r * rows + m * part, part), features_at],
                    update_out.at[r, m],
                )
                for m in range(rows // part)
            ]
            for r in range(steps)
        ]
        for copy in loads:
            copy.start()
        for copy in loads:
            copy.wait()
        first_scale = 1.0 / (1.0 - 0.9**STEP)
        second_scale = 1.0 / (1.0 - 0.999**STEP)
        for m in range(len(grads)):
            at = pl.ds(m * chunk, chunk)
            mine, others = grad_refs[2 * m][...], grad_refs[2 * m + 1][...]
            for h in range(2):
                here = pl.ds(h * half, half)
                grad_low = jnp.where(w[1] == h, mine, others).T.astype(F32)
                first_new = 0.9 * moment[0, at, here] + 0.1 * grad_low
                second_new = 0.999 * moment[1, at, here] + 0.001 * grad_low * grad_low
                moment[0, at, here] = first_new
                moment[1, at, here] = second_new
                ratio = (first_new * first_scale) / (
                    jnp.sqrt(second_new * second_scale) + 1e-08
                )
                direction[here, at] = ratio.astype(BF16).T
        for copy in stores:
            copy.start()
        for r in range(steps):
            at = pl.ds(r * rows, rows)
            out[at, :] = jnp.dot(
                own[at, :], direction[own_rows, :], preferred_element_type=F32
            ) + jnp.dot(other[at, :], direction[other_rows, :], preferred_element_type=F32)
            for copy in update_stores[r]:
                copy.start()
        for copy in stores + sum(update_stores, []):
            copy.wait()

    inputs = [*flat, own_proj, other_proj, *moments]
    any_space = pl.BlockSpec(memory_space=pl.ANY)
    in_specs = [whole(x) for x in (*flat, own_proj, other_proj)] + [any_space] * 2
    aliases = {}
    if before is not None:
        aliases = {1 + len(inputs) + n: n for n in range(3)}
        inputs += before
        in_specs += [any_space] * 3
    return pl.pallas_call(
        body,
        out_shape=[jax.ShapeDtypeStruct(x.shape, F32) for x in moments]
        + [jax.ShapeDtypeStruct((width, features), F32)],
        grid_spec=pltpu.PrefetchScalarGridSpec(
            num_scalar_prefetch=1,
            grid=(1,),
            in_specs=in_specs,
            out_specs=[any_space] * 3,
            scratch_shapes=[
                pltpu.VMEM((2, span, rank), F32),
                pltpu.VMEM((rank, span), BF16),
                pltpu.VMEM((width, span), F32),
                pltpu.SemaphoreType.DMA((2,)),
                pltpu.SemaphoreType.DMA((2,)),
                pltpu.SemaphoreType.DMA((steps, rows // part)),
            ],
        ),
        input_output_aliases=aliases,
        compiler_params=pltpu.CompilerParams(vmem_limit_bytes=28 * MIB),
        cost_estimate=busy(6),
        name="update_step",
    )(where, *inputs)


def in_vmem(x):
    return pltpu.with_memory_space_constraint(x, pltpu.VMEM)


def after(x, *others):
    return lax.optimization_barrier((x, *others))[0]


def add_up(arrays):
    return functools.reduce(jnp.add, [x.astype(F32) for x in arrays]).astype(BF16)


def on_device(dp, fsdp, acts, cotangent, projector, first_moment, second_moment):
    rows, rank = projector.shape
    half = rank // CORES
    groups = dp // CORES
    pieces = 2 if groups % 2 == 0 else 1
    span = rows // pieces
    chunk = span // 2 if span % 256 == 0 else span
    chunks = range(span // chunk)
    fsdp_at = lax.axis_index("fsdp").astype(jnp.int32)
    dp_at = lax.axis_index("dp")
    core_at = (dp_at % CORES).astype(jnp.int32)
    piece_at = ((dp_at // CORES) % pieces).astype(jnp.int32)
    where = jnp.stack([fsdp_at, core_at, piece_at])

    def to_core(x):
        return lax.ppermute(x, "dp", [(i, i ^ 1) for i in range(dp)])

    def to_fsdp(x, s):
        return lax.ppermute(x, "fsdp", [(i, i ^ s) for i in range(fsdp)])

    def to_piece(x, k):
        pairs = []
        for i in range(dp):
            group, core = divmod(i, CORES)
            base = group - group % pieces
            pairs.append((i, (base + (group + k) % pieces) * CORES + core))
        return lax.ppermute(x, "dp", pairs)

    def to_base(x, k):
        return lax.ppermute(x, "dp", [(i, (i + k * pieces * CORES) % dp) for i in range(dp)])

    def links(s):
        return (s & -s, 1 << (s.bit_length() - 1))

    levels = [
        [s for s in range(fsdp) if s.bit_count() == n] for n in range(fsdp.bit_length())
    ]

    part = rows // 2
    own_half, cot_out = cut_out(
        fsdp_at[None], core_at[None], piece_at[None], projector, cotangent, fsdp, pieces
    )
    held = {0: [(0, 0, own_half)]}
    for level in levels[1:]:
        for s in level:
            if s.bit_count() == 1:
                held[s] = [(s, 0, to_fsdp(own_half, s))]
                continue
            held[s] = []
            for n, link in enumerate(links(s)):
                source = held[s ^ link]
                x = source[n][2] if len(source) > 1 else source[0][2][n * part : (n + 1) * part]
                held[s].append((s, n * part, to_fsdp(x, link)))
    acts_pair = [acts, in_vmem(to_core(acts))]
    cots = [(cotangent, False), (in_vmem(to_core(after(cotangent, own_half))), False)]

    total = None
    for n, level in enumerate(levels):
        entries = [x for s in level for x in held[s]]
        last = n == len(levels) - 1
        total = coords_step(where, acts_pair, entries, total, rows, last, f"coords_{n}")
    full = [(0, half)]
    entries = [(s, 0, 0, [], full) for s in range(fsdp)]
    far_coords = None
    if pieces > 1:
        far_coords = to_piece(total, 1)
    sums = terms_step(
        where, cots, total, entries, pieces, span, span, "terms_chip", F32, 12
    )
    landed = {s: [(0, x)] for s, x in enumerate(sums)}
    cots_far = []
    if pieces > 1:
        arrived = after(to_piece(cot_out, 1), total)
        cots_far = [(arrived, True), (in_vmem(to_core(arrived)), True)]
        entries = [(0, 1, 0, [], full)]
        (pair_sum,) = terms_step(
            where, cots, total, entries, pieces, span, span, "terms_pair"
        )
        landed[0].append((0, to_piece(pair_sum, 1)))

    middle = half // 2
    halves = [(0, middle), (middle, half)]
    for n in range(len(levels) - 1, 1, -1):
        entries = [(s, 0, 0, landed[s], halves) for s in levels[n]]
        outs = iter(
            terms_step(
                where, cots_far, far_coords, entries, pieces, span, span, f"terms_{n}"
            )
        )
        for s in levels[n]:
            for m, link in enumerate(links(s)):
                landed[s ^ link].append((m * middle, to_fsdp(next(outs), link)))
    near = {j: [] for j in chunks}
    if fsdp > 1:
        entries = [(s, 0, j, landed[s], full) for j in chunks for s in levels[1]]
        outs = terms_step(
            where, cots_far, far_coords, entries, pieces, span, chunk, "terms_1"
        )
        for (s, _, j, _, _), x in zip(entries, outs):
            near[j].append((0, to_fsdp(x, s)))
    parts = []
    for j in chunks:
        entries = [(0, 0, j, landed[0] + near[j], full)]
        (x,) = terms_step(where, [], None, entries, pieces, span, chunk, "terms_0", BF16, 1)
        parts.append([x] + [to_base(x, k) for k in range(1, groups // pieces)])

    blocks = [(s, low, after(x, total)) for s in range(fsdp) for s, low, x in held[s]]
    own_proj = assemble(where, blocks, rows, fsdp)
    other_proj = to_core(own_proj)
    common = (own_proj, other_proj, (first_moment, second_moment))
    mine = jnp.concatenate([add_up(x) for x in parts], axis=1)
    outputs = update_step(where, 0, pieces, 0, [(mine, to_core(mine))], *common, None)
    if pieces > 1:
        others = to_piece(mine, 1)
        pair = (others, to_core(after(others, *outputs)))
        outputs = update_step(where, 1, pieces, 0, [pair], *common, outputs)
    return tuple(outputs)


def solution(mesh):
    in_specs = (
        P(("dp", "fsdp"), None),
        P(("dp", "fsdp"), None),
        P("fsdp", None),
        P("fsdp", None),
        P("fsdp", None),
    )
    out_specs = (P("fsdp", None), P("fsdp", None), P(None, "fsdp"))
    body = functools.partial(on_device, mesh.shape["dp"], mesh.shape["fsdp"])
    return jax.shard_map(body, mesh=mesh, in_specs=in_specs, out_specs=out_specs, check_vma=False)
```

```python
import functools

import jax
import jax.numpy as jnp
from jax import lax
from jax.experimental import pallas as pl
from jax.experimental.pallas import tpu as pltpu
from jax.sharding import PartitionSpec as P

STEP = 2
CORES = 2
MIB = 1024 * 1024
BF16 = jnp.bfloat16
F32 = jnp.float32


def cost(flops, bytes_accessed):
    return pl.CostEstimate(flops=flops, bytes_accessed=bytes_accessed, transcendentals=0)


def busy(us):
    return cost(int(us * 1.15e9), 0)


def whole(array):
    zeros = (0,) * array.ndim
    return pl.BlockSpec(array.shape, lambda i, w: zeros)


def call(body, where, inputs, in_specs, out_shape, limit, scratch=(), name=None, estimate=None):
    return pl.pallas_call(
        body,
        out_shape=out_shape,
        grid_spec=pltpu.PrefetchScalarGridSpec(
            num_scalar_prefetch=1,
            grid=(1,),
            in_specs=in_specs,
            out_specs=[whole(x) for x in out_shape],
            scratch_shapes=scratch,
        ),
        compiler_params=pltpu.CompilerParams(vmem_limit_bytes=limit),
        cost_estimate=estimate,
        name=name,
    )(where, *inputs)


def cut_out(fsdp_at, core, piece, projector, cotangent, fsdp, pieces):
    rows, rank = projector.shape
    half = rank // CORES
    tokens, width = cotangent.shape
    span = width // (fsdp * pieces)
    steps = 4

    def body(fsdp_ref, core_ref, piece_ref, proj_ref, cot_ref, proj_out, cot_out, sems):
        copies = []
        for s in range(1, fsdp):
            block = (fsdp_ref[0] ^ s) * pieces + pieces - 1 - piece_ref[0]
            source = cot_ref.at[:, pl.ds(pl.multiple_of(block * span, span), span)]
            copies.append((source, cot_out.at[:, pl.ds((s - 1) * span, span)]))
        columns = pl.ds(pl.multiple_of(core_ref[0] * half, half), half)
        for n in range(steps):
            at = pl.ds(n * (rows // steps), rows // steps)
            copies.append((proj_ref.at[at, columns], proj_out.at[at, :]))
        copies = [pltpu.make_async_copy(x, y, sems.at[n]) for n, (x, y) in enumerate(copies)]
        for copy in copies:
            copy.start()
        for copy in copies:
            copy.wait()

    hbm = [pltpu.with_memory_space_constraint(x, pltpu.HBM) for x in (projector, cotangent)]
    return pl.pallas_call(
        body,
        out_shape=[
            jax.ShapeDtypeStruct((rows, half), BF16),
            jax.ShapeDtypeStruct((tokens, (fsdp - 1) * span), BF16),
        ],
        in_specs=[pl.BlockSpec(memory_space=pltpu.SMEM)] * 3
        + [pl.BlockSpec(memory_space=pl.ANY)] * 2,
        out_specs=[pl.BlockSpec(memory_space=pltpu.VMEM)] * 2,
        scratch_shapes=[pltpu.SemaphoreType.DMA((fsdp + steps,))],
        compiler_params=pltpu.CompilerParams(vmem_limit_bytes=8 * MIB),
        cost_estimate=busy(1),
        name="cut_out",
    )(fsdp_at, core, piece, *hbm)


def coords_step(where, acts, proj, total, rows, last, name):
    tokens = acts[0].shape[0]
    half = proj[0][2].shape[1]
    inputs, specs = [], []
    for s, low, block in proj:
        size = block.shape[0]
        at = functools.partial(
            lambda s, low, size, i, w: (0, ((w[0] ^ s) * rows + low) // size), s, low, size
        )
        inputs += [*acts, block]
        specs += [pl.BlockSpec((tokens, size), at)] * 2 + [whole(block)]
    if total is not None:
        inputs.append(total)
        specs.append(whole(total))
    if last:
        shape = jax.ShapeDtypeStruct((half, 2 * tokens), BF16)
    else:
        shape = jax.ShapeDtypeStruct((2 * tokens, half), F32)

    def body(w, *refs):
        out = refs[len(inputs)]
        for t in range(2):
            span = slice(t * tokens, (t + 1) * tokens)
            value = None if total is None else refs[3 * len(proj)][span, :]
            for n in range(len(proj)):
                part = jnp.dot(
                    refs[3 * n + t][...], refs[3 * n + 2][...], preferred_element_type=F32
                )
                value = part if value is None else value + part
            if last:
                out[:, span] = value.T.astype(BF16)
            else:
                out[span, :] = value

    return call(
        body,
        where,
        inputs,
        specs,
        [shape],
        16 * MIB,
        name=name,
        estimate=busy(8),
    )[0]


def terms_step(where, cots, coords, entries, pieces, span, chunk, name, kind=BF16, estimate=1):
    per_piece = span // chunk
    half = entries[0][4][-1][1]
    inputs = [] if coords is None else [coords]
    specs = [whole(x) for x in inputs]
    out_shape = []
    for s, other, j, added, cuts in entries:
        for x, packed in cots:
            if packed and s == 0:
                continue

            def at(i, w, s=s, other=other, j=j, packed=packed):
                if packed:
                    return (0, (s - 1) * per_piece + j)
                piece = lax.rem(w[2] + other, pieces)
                return (0, ((w[0] ^ s) * pieces + piece) * per_piece + j)

            inputs.append(x)
            specs.append(pl.BlockSpec((x.shape[0], chunk), at))
        for _, x in added:
            column = j if x.shape[1] > chunk else 0
            at = functools.partial(lambda c, i, w: (0, c), column)
            inputs.append(x)
            specs.append(pl.BlockSpec((x.shape[0], chunk), at))
        out_shape += [jax.ShapeDtypeStruct((b - a, chunk), kind) for a, b in cuts]

    def body(w, *refs):
        ins = iter(refs[: len(inputs)])
        outs = iter(refs[len(inputs) : len(inputs) + len(out_shape)])
        value = refs[-1]
        coords_ref = None if coords is None else next(ins)
        for s, _, _, added, cuts in entries:
            term = None
            for n, (x, packed) in enumerate(cots):
                if packed and s == 0:
                    continue
                tokens = x.shape[0]
                part = jnp.dot(
                    coords_ref[:, n * tokens : (n + 1) * tokens],
                    next(ins)[...],
                    preferred_element_type=F32,
                )
                term = part if term is None else term + part
            extra = [(low, x.shape[0], next(ins)) for low, x in added]
            for low, size, ref in extra:
                if size == half:
                    part = ref[...].astype(F32)
                    term = part if term is None else term + part
            value[...] = term
            for low, size, ref in extra:
                if size < half:
                    value[low : low + size, :] += ref[...].astype(F32)
            for a, b in cuts:
                next(outs)[...] = value[a:b, :].astype(kind)

    return call(
        body,
        where,
        inputs,
        specs,
        out_shape,
        20 * MIB,
        scratch=[pltpu.VMEM((half, chunk), F32)],
        name=name,
        estimate=busy(estimate),
    )


def assemble(where, blocks, rows, parts):
    half = blocks[0][2].shape[1]
    inputs = [x for _, _, x in blocks]

    def body(w, *refs):
        out, sems = refs[-2:]
        copies = []
        for n, (s, low, x) in enumerate(blocks):
            size = x.shape[0]
            at = pl.ds(pl.multiple_of((w[0] ^ s) * rows + low, size), size)
            copies.append(pltpu.make_async_copy(refs[n], out.at[at, :], sems.at[n]))
        for copy in copies:
            copy.start()
        for copy in copies:
            copy.wait()

    return pl.pallas_call(
        body,
        out_shape=jax.ShapeDtypeStruct((parts * rows, half), BF16),
        in_specs=[pl.BlockSpec(memory_space=pltpu.SMEM)]
        + [pl.BlockSpec(memory_space=pl.ANY)] * len(inputs),
        out_specs=pl.BlockSpec(memory_space=pl.ANY),
        scratch_shapes=[pltpu.SemaphoreType.DMA((len(inputs),))],
        compiler_params=pltpu.CompilerParams(vmem_limit_bytes=4 * MIB),
        cost_estimate=busy(2),
        name="assemble",
    )(where, *inputs)


def join(where, own, other):
    width, half = own.shape

    def body(w, own_ref, other_ref, out):
        @pl.when(w[1] == 0)
        def _():
            out[:, :half] = own_ref[...]
            out[:, half:] = other_ref[...]

        @pl.when(w[1] != 0)
        def _():
            out[:, :half] = other_ref[...]
            out[:, half:] = own_ref[...]

    return call(
        body,
        where,
        [own, other],
        [whole(own), whole(other)],
        [jax.ShapeDtypeStruct((width, 2 * half), BF16)],
        20 * MIB,
        name="join",
        estimate=busy(1),
    )[0]


def update_step(where, k, pieces, grads, proj, moments, before):
    half, span = grads[0].shape
    rank = CORES * half
    features = moments[0].shape[0]
    width = proj.shape[0]
    rows = min(1024, width)
    steps = width // rows
    some = 16

    def piece(w):
        return lax.rem(w[2] + pieces - k, pieces)

    def body(w, own, other, proj_ref, first_ref, second_ref, *refs):
        outs, update = refs[-10:-8], refs[-8]
        moment, grad, ratio, direction, out = refs[-7:-2]
        moment_out, update_out = refs[-2:]
        features_at = pl.ds(pl.multiple_of(piece(w) * span, span), span)
        stores = [
            pltpu.make_async_copy(moment.at[n], outs[n].at[features_at, :], moment_out.at[n])
            for n in range(2)
        ]
        update_stores = [
            pltpu.make_async_copy(
                out.at[pl.ds(r * rows, rows), :],
                update.at[pl.ds(r * rows, rows), features_at],
                update_out.at[r],
            )
            for r in range(steps)
        ]
        for h in range(2):
            grad[:, pl.ds(h * half, half)] = jnp.where(w[1] == h, own[...], other[...]).T
        first_scale = 1.0 / (1.0 - 0.9**STEP)
        second_scale = 1.0 / (1.0 - 0.999**STEP)

        def adam(n, _):
            at = pl.ds(pl.multiple_of(n * some, some), some)
            grad_low = grad[at, :].astype(F32)
            first_new = 0.9 * first_ref[at, :] + 0.1 * grad_low
            second_new = 0.999 * second_ref[at, :] + 0.001 * grad_low * grad_low
            moment[0, at, :] = first_new
            moment[1, at, :] = second_new
            ratio[at, :] = (
                (first_new * first_scale) / (jnp.sqrt(second_new * second_scale) + 1e-08)
            ).astype(BF16)
            return 0

        lax.fori_loop(0, span // some, adam, 0, unroll=2)
        for copy in stores:
            copy.start()
        direction[...] = ratio[...].T
        for r in range(steps):
            at = pl.ds(r * rows, rows)
            out[at, :] = jnp.dot(proj_ref[at, :], direction[...], preferred_element_type=F32)
            update_stores[r].start()
        for copy in stores + update_stores:
            copy.wait()

    inputs = [*grads, proj, *moments]
    any_space = pl.BlockSpec(memory_space=pl.ANY)
    in_specs = [whole(x) for x in (*grads, proj)]
    in_specs += [pl.BlockSpec((span, rank), lambda i, w: (piece(w), 0))] * 2
    aliases = {}
    if before is not None:
        aliases = {1 + len(inputs) + n: n for n in range(3)}
        inputs += before
        in_specs += [any_space] * 3
    return pl.pallas_call(
        body,
        out_shape=[jax.ShapeDtypeStruct(x.shape, F32) for x in moments]
        + [jax.ShapeDtypeStruct((width, features), F32)],
        grid_spec=pltpu.PrefetchScalarGridSpec(
            num_scalar_prefetch=1,
            grid=(1,),
            in_specs=in_specs,
            out_specs=[any_space] * 3,
            scratch_shapes=[
                pltpu.VMEM((2, span, rank), F32),
                pltpu.VMEM((span, rank), BF16),
                pltpu.VMEM((span, rank), BF16),
                pltpu.VMEM((rank, span), BF16),
                pltpu.VMEM((width, span), F32),
                pltpu.SemaphoreType.DMA((2,)),
                pltpu.SemaphoreType.DMA((steps,)),
            ],
        ),
        input_output_aliases=aliases,
        compiler_params=pltpu.CompilerParams(vmem_limit_bytes=28 * MIB),
        cost_estimate=busy(6),
        name="update_step",
    )(where, *inputs)


def in_vmem(x):
    return pltpu.with_memory_space_constraint(x, pltpu.VMEM)


def after(x, *others):
    return lax.optimization_barrier((x, *others))[0]


def add_up(arrays):
    return functools.reduce(jnp.add, [x.astype(F32) for x in arrays]).astype(BF16)


def on_device(dp, fsdp, acts, cotangent, projector, first_moment, second_moment):
    rows, rank = projector.shape
    half = rank // CORES
    groups = dp // CORES
    pieces = 2 if groups % 2 == 0 else 1
    span = rows // pieces
    chunk = span // 2 if span % 256 == 0 else span
    chunks = range(span // chunk)
    fsdp_at = lax.axis_index("fsdp").astype(jnp.int32)
    dp_at = lax.axis_index("dp")
    core_at = (dp_at % CORES).astype(jnp.int32)
    piece_at = ((dp_at // CORES) % pieces).astype(jnp.int32)
    where = jnp.stack([fsdp_at, core_at, piece_at])

    def to_core(x):
        return lax.ppermute(x, "dp", [(i, i ^ 1) for i in range(dp)])

    def to_fsdp(x, s):
        return lax.ppermute(x, "fsdp", [(i, i ^ s) for i in range(fsdp)])

    def to_piece(x, k):
        pairs = []
        for i in range(dp):
            group, core = divmod(i, CORES)
            base = group - group % pieces
            pairs.append((i, (base + (group + k) % pieces) * CORES + core))
        return lax.ppermute(x, "dp", pairs)

    def to_base(x, k):
        return lax.ppermute(x, "dp", [(i, (i + k * pieces * CORES) % dp) for i in range(dp)])

    def links(s):
        return (s & -s, 1 << (s.bit_length() - 1))

    levels = [
        [s for s in range(fsdp) if s.bit_count() == n] for n in range(fsdp.bit_length())
    ]

    part = rows // 2
    own_half, cot_out = cut_out(
        fsdp_at[None], core_at[None], piece_at[None], projector, cotangent, fsdp, pieces
    )
    held = {0: [(0, 0, own_half)]}
    for level in levels[1:]:
        for s in level:
            if s.bit_count() == 1:
                held[s] = [(s, 0, to_fsdp(own_half, s))]
                continue
            held[s] = []
            for n, link in enumerate(links(s)):
                source = held[s ^ link]
                x = source[n][2] if len(source) > 1 else source[0][2][n * part : (n + 1) * part]
                held[s].append((s, n * part, to_fsdp(x, link)))
    acts_pair = [acts, in_vmem(to_core(acts))]
    cots = [(cotangent, False), (in_vmem(to_core(after(cotangent, own_half))), False)]

    total = None
    for n, level in enumerate(levels):
        entries = [x for s in level for x in held[s]]
        last = n == len(levels) - 1
        total = coords_step(where, acts_pair, entries, total, rows, last, f"coords_{n}")
    full = [(0, half)]
    entries = [(s, 0, 0, [], full) for s in range(fsdp)]
    far_coords = None
    if pieces > 1:
        far_coords = to_piece(total, 1)
    sums = terms_step(
        where, cots, total, entries, pieces, span, span, "terms_chip", F32, 12
    )
    landed = {s: [(0, x)] for s, x in enumerate(sums)}
    cots_far = []
    if pieces > 1:
        arrived = after(to_piece(cot_out, 1), total)
        cots_far = [(arrived, True), (in_vmem(to_core(arrived)), True)]
        entries = [(0, 1, 0, [], full)]
        (pair_sum,) = terms_step(
            where, cots, total, entries, pieces, span, span, "terms_pair"
        )
        landed[0].append((0, to_piece(pair_sum, 1)))

    got = {j: list(landed[0]) for j in chunks}
    if fsdp > 1:
        entries = [
            (s, 0, j, landed[s], full) for j in chunks for s in range(fsdp - 1, 0, -1)
        ]
        outs = terms_step(
            where, cots_far, after(far_coords, pair_sum), entries, pieces, span, chunk, "terms_peers", BF16, 8
        )
        for (s, _, j, _, _), x in zip(entries, outs):
            got[j].append((0, to_fsdp(x, s)))
    parts = []
    for j in chunks:
        entries = [(0, 0, j, got[j], full)]
        (x,) = terms_step(where, [], None, entries, pieces, span, chunk, "terms_own")
        parts.append([x] + [to_base(x, k) for k in range(1, groups // pieces)])

    blocks = [(s, low, after(x, total)) for s in range(fsdp) for s, low, x in held[s]]
    own_proj = assemble(where, blocks, rows, fsdp)
    other_proj = to_core(own_proj)
    proj = join(where, own_proj, after(other_proj, total))
    moments = (first_moment, second_moment)
    parts[0] = [after(x, proj) for x in parts[0]]
    mine = jnp.concatenate([add_up(x) for x in parts], axis=1)
    outputs = update_step(where, 0, pieces, (mine, to_core(mine)), proj, moments, None)
    if pieces > 1:
        others = to_piece(mine, 1)
        pair = (others, to_core(after(others, *outputs)))
        outputs = update_step(where, 1, pieces, pair, proj, moments, outputs)
    return tuple(outputs)


def solution(mesh):
    in_specs = (
        P(("dp", "fsdp"), None),
        P(("dp", "fsdp"), None),
        P("fsdp", None),
        P("fsdp", None),
        P("fsdp", None),
    )
    out_specs = (P("fsdp", None), P("fsdp", None), P(None, "fsdp"))
    body = functools.partial(on_device, mesh.shape["dp"], mesh.shape["fsdp"])
    return jax.shard_map(body, mesh=mesh, in_specs=in_specs, out_specs=out_specs, check_vma=False)
```

```python
import functools

import jax
import jax.numpy as jnp
from jax import lax
from jax.experimental import pallas as pl
from jax.experimental.pallas import tpu as pltpu
from jax.sharding import PartitionSpec as P

STEP = 2
CORES = 2
MIB = 1024 * 1024
BF16 = jnp.bfloat16
F32 = jnp.float32


def cost(flops, bytes_accessed):
    return pl.CostEstimate(flops=flops, bytes_accessed=bytes_accessed, transcendentals=0)


def busy(us):
    return cost(int(us * 1.15e9), 0)


def whole(array):
    zeros = (0,) * array.ndim
    return pl.BlockSpec(array.shape, lambda i, w: zeros)


def call(body, where, inputs, in_specs, out_shape, limit, scratch=(), name=None, estimate=None):
    return pl.pallas_call(
        body,
        out_shape=out_shape,
        grid_spec=pltpu.PrefetchScalarGridSpec(
            num_scalar_prefetch=1,
            grid=(1,),
            in_specs=in_specs,
            out_specs=[whole(x) for x in out_shape],
            scratch_shapes=scratch,
        ),
        compiler_params=pltpu.CompilerParams(vmem_limit_bytes=limit),
        cost_estimate=estimate,
        name=name,
    )(where, *inputs)


def cut_out(fsdp_at, core, piece, projector, cotangent, fsdp, pieces):
    rows, rank = projector.shape
    half = rank // CORES
    tokens, width = cotangent.shape
    span = width // (fsdp * pieces)
    steps = 4

    def body(fsdp_ref, core_ref, piece_ref, proj_ref, cot_ref, proj_out, cot_out, sems):
        copies = []
        for s in range(1, fsdp):
            block = (fsdp_ref[0] ^ s) * pieces + pieces - 1 - piece_ref[0]
            source = cot_ref.at[:, pl.ds(pl.multiple_of(block * span, span), span)]
            copies.append((source, cot_out.at[:, pl.ds((s - 1) * span, span)]))
        columns = pl.ds(pl.multiple_of(core_ref[0] * half, half), half)
        for n in range(steps):
            at = pl.ds(n * (rows // steps), rows // steps)
            copies.append((proj_ref.at[at, columns], proj_out.at[at, :]))
        copies = [pltpu.make_async_copy(x, y, sems.at[n]) for n, (x, y) in enumerate(copies)]
        for copy in copies:
            copy.start()
        for copy in copies:
            copy.wait()

    hbm = [pltpu.with_memory_space_constraint(x, pltpu.HBM) for x in (projector, cotangent)]
    return pl.pallas_call(
        body,
        out_shape=[
            jax.ShapeDtypeStruct((rows, half), BF16),
            jax.ShapeDtypeStruct((tokens, (fsdp - 1) * span), BF16),
        ],
        in_specs=[pl.BlockSpec(memory_space=pltpu.SMEM)] * 3
        + [pl.BlockSpec(memory_space=pl.ANY)] * 2,
        out_specs=[pl.BlockSpec(memory_space=pltpu.VMEM)] * 2,
        scratch_shapes=[pltpu.SemaphoreType.DMA((fsdp + steps,))],
        compiler_params=pltpu.CompilerParams(vmem_limit_bytes=8 * MIB),
        cost_estimate=busy(1),
        name="cut_out",
    )(fsdp_at, core, piece, *hbm)


def coords_step(where, acts, proj, total, rows, last, name):
    tokens = acts[0].shape[0]
    half = proj[0][2].shape[1]
    inputs, specs = [], []
    for s, low, block in proj:
        size = block.shape[0]
        at = functools.partial(
            lambda s, low, size, i, w: (0, ((w[0] ^ s) * rows + low) // size), s, low, size
        )
        inputs += [*acts, block]
        specs += [pl.BlockSpec((tokens, size), at)] * 2 + [whole(block)]
    if total is not None:
        inputs.append(total)
        specs.append(whole(total))
    if last:
        shape = jax.ShapeDtypeStruct((half, 2 * tokens), BF16)
    else:
        shape = jax.ShapeDtypeStruct((2 * tokens, half), F32)

    def body(w, *refs):
        out = refs[len(inputs)]
        for t in range(2):
            span = slice(t * tokens, (t + 1) * tokens)
            value = None if total is None else refs[3 * len(proj)][span, :]
            for n in range(len(proj)):
                part = jnp.dot(
                    refs[3 * n + t][...], refs[3 * n + 2][...], preferred_element_type=F32
                )
                value = part if value is None else value + part
            if last:
                out[:, span] = value.T.astype(BF16)
            else:
                out[span, :] = value

    return call(
        body,
        where,
        inputs,
        specs,
        [shape],
        16 * MIB,
        name=name,
        estimate=busy(8),
    )[0]


def terms_step(where, cots, coords, entries, pieces, span, chunk, name, kind=BF16, estimate=1):
    per_piece = span // chunk
    half = entries[0][4][-1][1]
    inputs = [] if coords is None else [coords]
    specs = [whole(x) for x in inputs]
    out_shape = []
    for s, other, j, added, cuts in entries:
        for x, packed in cots:
            if packed and s == 0:
                continue

            def at(i, w, s=s, other=other, j=j, packed=packed):
                if packed:
                    return (0, (s - 1) * per_piece + j)
                piece = lax.rem(w[2] + other, pieces)
                return (0, ((w[0] ^ s) * pieces + piece) * per_piece + j)

            inputs.append(x)
            specs.append(pl.BlockSpec((x.shape[0], chunk), at))
        for _, x in added:
            column = j if x.shape[1] > chunk else 0
            at = functools.partial(lambda c, i, w: (0, c), column)
            inputs.append(x)
            specs.append(pl.BlockSpec((x.shape[0], chunk), at))
        out_shape += [jax.ShapeDtypeStruct((b - a, chunk), kind) for a, b in cuts]

    def body(w, *refs):
        ins = iter(refs[: len(inputs)])
        outs = iter(refs[len(inputs) : len(inputs) + len(out_shape)])
        value = refs[-1]
        coords_ref = None if coords is None else next(ins)
        for s, _, _, added, cuts in entries:
            term = None
            for n, (x, packed) in enumerate(cots):
                if packed and s == 0:
                    continue
                tokens = x.shape[0]
                part = jnp.dot(
                    coords_ref[:, n * tokens : (n + 1) * tokens],
                    next(ins)[...],
                    preferred_element_type=F32,
                )
                term = part if term is None else term + part
            extra = [(low, x.shape[0], next(ins)) for low, x in added]
            for low, size, ref in extra:
                if size == half:
                    part = ref[...].astype(F32)
                    term = part if term is None else term + part
            value[...] = term
            for low, size, ref in extra:
                if size < half:
                    value[low : low + size, :] += ref[...].astype(F32)
            for a, b in cuts:
                next(outs)[...] = value[a:b, :].astype(kind)

    return call(
        body,
        where,
        inputs,
        specs,
        out_shape,
        20 * MIB,
        scratch=[pltpu.VMEM((half, chunk), F32)],
        name=name,
        estimate=busy(estimate),
    )


def assemble(where, blocks, rows, parts):
    half = blocks[0][2].shape[1]
    inputs = [x for _, _, x in blocks]

    def body(w, *refs):
        out, sems = refs[-2:]
        copies = []
        for n, (s, low, x) in enumerate(blocks):
            size = x.shape[0]
            at = pl.ds(pl.multiple_of((w[0] ^ s) * rows + low, size), size)
            copies.append(pltpu.make_async_copy(refs[n], out.at[at, :], sems.at[n]))
        for copy in copies:
            copy.start()
        for copy in copies:
            copy.wait()

    return pl.pallas_call(
        body,
        out_shape=jax.ShapeDtypeStruct((parts * rows, half), BF16),
        in_specs=[pl.BlockSpec(memory_space=pltpu.SMEM)]
        + [pl.BlockSpec(memory_space=pl.ANY)] * len(inputs),
        out_specs=pl.BlockSpec(memory_space=pl.ANY),
        scratch_shapes=[pltpu.SemaphoreType.DMA((len(inputs),))],
        compiler_params=pltpu.CompilerParams(vmem_limit_bytes=4 * MIB),
        cost_estimate=busy(2),
        name="assemble",
    )(where, *inputs)


def join(where, own, other):
    width, half = own.shape

    def body(w, own_ref, other_ref, out):
        @pl.when(w[1] == 0)
        def _():
            out[:, :half] = own_ref[...]
            out[:, half:] = other_ref[...]

        @pl.when(w[1] != 0)
        def _():
            out[:, :half] = other_ref[...]
            out[:, half:] = own_ref[...]

    return call(
        body,
        where,
        [own, other],
        [whole(own), whole(other)],
        [jax.ShapeDtypeStruct((width, 2 * half), BF16)],
        20 * MIB,
        name="join",
        estimate=busy(1),
    )[0]


def update_step(where, k, pieces, grads, proj, moments, before):
    half, span = grads[0].shape
    rank = CORES * half
    features = moments[0].shape[0]
    width = proj.shape[0]
    rows = min(512, width)
    steps = width // rows
    some = 16

    def piece(w):
        return lax.rem(w[2] + pieces - k, pieces)

    def body(w, own, *refs):
        others, (proj_ref, first_ref, second_ref) = refs[: len(grads) - 1], refs[len(grads) - 1 :][:3]
        outs, update = refs[-10:-8], refs[-8]
        moment, grad, ratio, direction, out = refs[-7:-2]
        moment_out, update_out = refs[-2:]
        features_at = pl.ds(pl.multiple_of(piece(w) * span, span), span)
        stores = [
            pltpu.make_async_copy(moment.at[n], outs[n].at[features_at, :], moment_out.at[n])
            for n in range(2)
        ]
        update_stores = [
            pltpu.make_async_copy(
                out.at[pl.ds(r * rows, rows), :],
                update.at[pl.ds(r * rows, rows), features_at],
                update_out.at[r],
            )
            for r in range(steps)
        ]
        for n, other in enumerate(others):
            size = other.shape[1]
            at = pl.ds(n * size, size)
            for h in range(2):
                part = jnp.where(w[1] == h, own[:, at], other[...])
                grad[at, pl.ds(h * half, half)] = part.T
        first_scale = 1.0 / (1.0 - 0.9**STEP)
        second_scale = 1.0 / (1.0 - 0.999**STEP)

        def adam(n, _):
            at = pl.ds(pl.multiple_of(n * some, some), some)
            grad_low = grad[at, :].astype(F32)
            first_new = 0.9 * first_ref[at, :] + 0.1 * grad_low
            second_new = 0.999 * second_ref[at, :] + 0.001 * grad_low * grad_low
            moment[0, at, :] = first_new
            moment[1, at, :] = second_new
            ratio[at, :] = (
                (first_new * first_scale) / (jnp.sqrt(second_new * second_scale) + 1e-08)
            ).astype(BF16)
            return 0

        lax.fori_loop(0, span // some, adam, 0, unroll=2)
        for copy in stores:
            copy.start()
        direction[...] = ratio[...].T
        for r in range(steps):
            at = pl.ds(r * rows, rows)
            out[at, :] = jnp.dot(proj_ref[at, :], direction[...], preferred_element_type=F32)
            update_stores[r].start()
        for copy in stores + update_stores:
            copy.wait()

    inputs = [*grads, proj, *moments]
    any_space = pl.BlockSpec(memory_space=pl.ANY)
    in_specs = [whole(x) for x in (*grads, proj)]
    in_specs += [pl.BlockSpec((span, rank), lambda i, w: (piece(w), 0))] * 2
    aliases = {}
    if before is not None:
        aliases = {1 + len(inputs) + n: n for n in range(3)}
        inputs += before
        in_specs += [any_space] * 3
    return pl.pallas_call(
        body,
        out_shape=[jax.ShapeDtypeStruct(x.shape, F32) for x in moments]
        + [jax.ShapeDtypeStruct((width, features), F32)],
        grid_spec=pltpu.PrefetchScalarGridSpec(
            num_scalar_prefetch=1,
            grid=(1,),
            in_specs=in_specs,
            out_specs=[any_space] * 3,
            scratch_shapes=[
                pltpu.VMEM((2, span, rank), F32),
                pltpu.VMEM((span, rank), BF16),
                pltpu.VMEM((span, rank), BF16),
                pltpu.VMEM((rank, span), BF16),
                pltpu.VMEM((width, span), F32),
                pltpu.SemaphoreType.DMA((2,)),
                pltpu.SemaphoreType.DMA((steps,)),
            ],
        ),
        input_output_aliases=aliases,
        compiler_params=pltpu.CompilerParams(vmem_limit_bytes=28 * MIB),
        cost_estimate=busy(0.5),
        name="update_step",
    )(where, *inputs)


def in_vmem(x):
    return pltpu.with_memory_space_constraint(x, pltpu.VMEM)


def after(x, *others):
    return lax.optimization_barrier((x, *others))[0]


def add_up(arrays):
    return functools.reduce(jnp.add, [x.astype(F32) for x in arrays]).astype(BF16)


def on_device(dp, fsdp, acts, cotangent, projector, first_moment, second_moment):
    rows, rank = projector.shape
    half = rank // CORES
    groups = dp // CORES
    pieces = 2 if groups % 2 == 0 else 1
    span = rows // pieces
    chunk = span // 2 if span % 256 == 0 else span
    chunks = range(span // chunk)
    fsdp_at = lax.axis_index("fsdp").astype(jnp.int32)
    dp_at = lax.axis_index("dp")
    core_at = (dp_at % CORES).astype(jnp.int32)
    piece_at = ((dp_at // CORES) % pieces).astype(jnp.int32)
    where = jnp.stack([fsdp_at, core_at, piece_at])

    def to_core(x):
        return lax.ppermute(x, "dp", [(i, i ^ 1) for i in range(dp)])

    def to_fsdp(x, s):
        return lax.ppermute(x, "fsdp", [(i, i ^ s) for i in range(fsdp)])

    def to_piece(x, k):
        pairs = []
        for i in range(dp):
            group, core = divmod(i, CORES)
            base = group - group % pieces
            pairs.append((i, (base + (group + k) % pieces) * CORES + core))
        return lax.ppermute(x, "dp", pairs)

    def to_base(x, k):
        return lax.ppermute(x, "dp", [(i, (i + k * pieces * CORES) % dp) for i in range(dp)])

    def links(s):
        return (s & -s, 1 << (s.bit_length() - 1))

    levels = [
        [s for s in range(fsdp) if s.bit_count() == n] for n in range(fsdp.bit_length())
    ]

    part = rows // 2
    own_half, cot_out = cut_out(
        fsdp_at[None], core_at[None], piece_at[None], projector, cotangent, fsdp, pieces
    )
    held = {0: [(0, 0, own_half)]}
    for level in levels[1:]:
        for s in level:
            if s.bit_count() == 1:
                held[s] = [(s, 0, to_fsdp(own_half, s))]
                continue
            held[s] = []
            for n, link in enumerate(links(s)):
                source = held[s ^ link]
                x = source[n][2] if len(source) > 1 else source[0][2][n * part : (n + 1) * part]
                held[s].append((s, n * part, to_fsdp(x, link)))
    acts_pair = [acts, in_vmem(to_core(acts))]
    cots = [(cotangent, False), (in_vmem(to_core(after(cotangent, own_half))), False)]

    total = None
    for n, level in enumerate(levels):
        entries = [x for s in level for x in held[s]]
        last = n == len(levels) - 1
        total = coords_step(where, acts_pair, entries, total, rows, last, f"coords_{n}")
    full = [(0, half)]
    entries = [(s, 0, 0, [], full) for s in range(fsdp)]
    far_coords = None
    if pieces > 1:
        far_coords = to_piece(total, 1)
    sums = terms_step(
        where, cots, total, entries, pieces, span, span, "terms_chip", F32, 12
    )
    landed = {s: [(0, x)] for s, x in enumerate(sums)}
    cots_far = []
    if pieces > 1:
        arrived = after(to_piece(cot_out, 1), total)
        cots_far = [(arrived, True), (in_vmem(to_core(arrived)), True)]
        entries = [(0, 1, 0, [], full)]
        (pair_sum,) = terms_step(
            where, cots, total, entries, pieces, span, span, "terms_pair"
        )
        landed[0].append((0, to_piece(pair_sum, 1)))

    middle = half // 2
    halves = [(0, middle), (middle, half)]
    for n in range(len(levels) - 1, 1, -1):
        entries = [(s, 0, 0, landed[s], halves) for s in levels[n]]
        outs = iter(
            terms_step(
                where, cots_far, far_coords, entries, pieces, span, span, f"terms_{n}"
            )
        )
        for s in levels[n]:
            for m, link in enumerate(links(s)):
                landed[s ^ link].append((m * middle, to_fsdp(next(outs), link)))
    near = {j: [] for j in chunks}
    if fsdp > 1:
        entries = [(s, 0, j, landed[s], full) for j in chunks for s in levels[1]]
        outs = terms_step(
            where, cots_far, far_coords, entries, pieces, span, chunk, "terms_1"
        )
        for (s, _, j, _, _), x in zip(entries, outs):
            near[j].append((0, to_fsdp(x, s)))
    parts = []
    for j in chunks:
        entries = [(0, 0, j, landed[0] + near[j], full)]
        (x,) = terms_step(where, [], None, entries, pieces, span, chunk, "terms_0", BF16, 1)
        parts.append([x] + [to_base(x, k) for k in range(1, groups // pieces)])

    blocks = [(s, low, after(x, total)) for s in range(fsdp) for s, low, x in held[s]]
    own_proj = assemble(where, blocks, rows, fsdp)
    other_proj = to_core(own_proj)
    proj = join(where, own_proj, after(other_proj, total))
    moments = (first_moment, second_moment)
    parts[0] = [after(x, proj) for x in parts[0]]
    sums, others = [], []
    for x in parts:
        sums.append(add_up([after(y, *others) for y in x]))
        others.append(to_core(sums[-1]))
    mine = jnp.concatenate(sums, axis=1)
    outputs = update_step(where, 0, pieces, (mine, *others), proj, moments, None)
    if pieces > 1:
        others = to_piece(mine, 1)
        pair = (others, to_core(after(others, *outputs)))
        outputs = update_step(where, 1, pieces, pair, proj, moments, outputs)
    return tuple(outputs)


def solution(mesh):
    in_specs = (
        P(("dp", "fsdp"), None),
        P(("dp", "fsdp"), None),
        P("fsdp", None),
        P("fsdp", None),
        P("fsdp", None),
    )
    out_specs = (P("fsdp", None), P("fsdp", None), P(None, "fsdp"))
    body = functools.partial(on_device, mesh.shape["dp"], mesh.shape["fsdp"])
    return jax.shard_map(body, mesh=mesh, in_specs=in_specs, out_specs=out_specs, check_vma=False)
```

```python
import functools

import jax
import jax.numpy as jnp
from jax import lax
from jax.experimental import pallas as pl
from jax.experimental.pallas import tpu as pltpu
from jax.sharding import PartitionSpec as P

STEP = 2
CORES = 2
MIB = 1024 * 1024
BF16 = jnp.bfloat16
F32 = jnp.float32


def cost(flops, bytes_accessed):
    return pl.CostEstimate(flops=flops, bytes_accessed=bytes_accessed, transcendentals=0)


def busy(us):
    return cost(int(us * 1.15e9), 0)


def whole(array):
    zeros = (0,) * array.ndim
    return pl.BlockSpec(array.shape, lambda i, w: zeros)


def call(body, where, inputs, in_specs, out_shape, limit, scratch=(), name=None, estimate=None):
    return pl.pallas_call(
        body,
        out_shape=out_shape,
        grid_spec=pltpu.PrefetchScalarGridSpec(
            num_scalar_prefetch=1,
            grid=(1,),
            in_specs=in_specs,
            out_specs=[whole(x) for x in out_shape],
            scratch_shapes=scratch,
        ),
        compiler_params=pltpu.CompilerParams(vmem_limit_bytes=limit),
        cost_estimate=estimate,
        name=name,
    )(where, *inputs)


def cut_out(fsdp_at, core, piece, projector, cotangent, fsdp, pieces):
    rows, rank = projector.shape
    half = rank // CORES
    tokens, width = cotangent.shape
    span = width // (fsdp * pieces)
    steps = 4

    def body(fsdp_ref, core_ref, piece_ref, proj_ref, cot_ref, proj_out, cot_out, sems):
        copies = []
        for s in range(1, fsdp):
            block = (fsdp_ref[0] ^ s) * pieces + pieces - 1 - piece_ref[0]
            source = cot_ref.at[:, pl.ds(pl.multiple_of(block * span, span), span)]
            copies.append((source, cot_out.at[:, pl.ds((s - 1) * span, span)]))
        columns = pl.ds(pl.multiple_of(core_ref[0] * half, half), half)
        for n in range(steps):
            at = pl.ds(n * (rows // steps), rows // steps)
            copies.append((proj_ref.at[at, columns], proj_out.at[at, :]))
        copies = [pltpu.make_async_copy(x, y, sems.at[n]) for n, (x, y) in enumerate(copies)]
        for copy in copies:
            copy.start()
        for copy in copies:
            copy.wait()

    hbm = [pltpu.with_memory_space_constraint(x, pltpu.HBM) for x in (projector, cotangent)]
    return pl.pallas_call(
        body,
        out_shape=[
            jax.ShapeDtypeStruct((rows, half), BF16),
            jax.ShapeDtypeStruct((tokens, (fsdp - 1) * span), BF16),
        ],
        in_specs=[pl.BlockSpec(memory_space=pltpu.SMEM)] * 3
        + [pl.BlockSpec(memory_space=pl.ANY)] * 2,
        out_specs=[pl.BlockSpec(memory_space=pltpu.VMEM)] * 2,
        scratch_shapes=[pltpu.SemaphoreType.DMA((fsdp + steps,))],
        compiler_params=pltpu.CompilerParams(vmem_limit_bytes=8 * MIB),
        cost_estimate=busy(1),
        name="cut_out",
    )(fsdp_at, core, piece, *hbm)


def coords_step(where, acts, proj, total, rows, last, name):
    tokens = acts[0].shape[0]
    half = proj[0][2].shape[1]
    inputs, specs = [], []
    for s, low, block in proj:
        size = block.shape[0]
        at = functools.partial(
            lambda s, low, size, i, w: (0, ((w[0] ^ s) * rows + low) // size), s, low, size
        )
        inputs += [*acts, block]
        specs += [pl.BlockSpec((tokens, size), at)] * 2 + [whole(block)]
    if total is not None:
        inputs.append(total)
        specs.append(whole(total))
    if last:
        shape = jax.ShapeDtypeStruct((half, 2 * tokens), BF16)
    else:
        shape = jax.ShapeDtypeStruct((2 * tokens, half), F32)

    def body(w, *refs):
        out = refs[len(inputs)]
        for t in range(2):
            span = slice(t * tokens, (t + 1) * tokens)
            value = None if total is None else refs[3 * len(proj)][span, :]
            for n in range(len(proj)):
                part = jnp.dot(
                    refs[3 * n + t][...], refs[3 * n + 2][...], preferred_element_type=F32
                )
                value = part if value is None else value + part
            if last:
                out[:, span] = value.T.astype(BF16)
            else:
                out[span, :] = value

    return call(
        body,
        where,
        inputs,
        specs,
        [shape],
        16 * MIB,
        name=name,
        estimate=busy(8),
    )[0]


def terms_step(where, cots, coords, entries, pieces, span, chunk, name, kind=BF16, estimate=1):
    per_piece = span // chunk
    half = entries[0][4][-1][1]
    inputs = [] if coords is None else [coords]
    specs = [whole(x) for x in inputs]
    out_shape = []
    for s, other, j, added, cuts in entries:
        for x, packed in cots:
            if packed and s == 0:
                continue

            def at(i, w, s=s, other=other, j=j, packed=packed):
                if packed:
                    return (0, (s - 1) * per_piece + j)
                piece = lax.rem(w[2] + other, pieces)
                return (0, ((w[0] ^ s) * pieces + piece) * per_piece + j)

            inputs.append(x)
            specs.append(pl.BlockSpec((x.shape[0], chunk), at))
        for _, x in added:
            column = j if x.shape[1] > chunk else 0
            at = functools.partial(lambda c, i, w: (0, c), column)
            inputs.append(x)
            specs.append(pl.BlockSpec((x.shape[0], chunk), at))
        out_shape += [jax.ShapeDtypeStruct((b - a, chunk), kind) for a, b in cuts]

    def body(w, *refs):
        ins = iter(refs[: len(inputs)])
        outs = iter(refs[len(inputs) : len(inputs) + len(out_shape)])
        value = refs[-1]
        coords_ref = None if coords is None else next(ins)
        for s, _, _, added, cuts in entries:
            term = None
            for n, (x, packed) in enumerate(cots):
                if packed and s == 0:
                    continue
                tokens = x.shape[0]
                part = jnp.dot(
                    coords_ref[:, n * tokens : (n + 1) * tokens],
                    next(ins)[...],
                    preferred_element_type=F32,
                )
                term = part if term is None else term + part
            extra = [(low, x.shape[0], next(ins)) for low, x in added]
            for low, size, ref in extra:
                if size == half:
                    part = ref[...].astype(F32)
                    term = part if term is None else term + part
            value[...] = term
            for low, size, ref in extra:
                if size < half:
                    value[low : low + size, :] += ref[...].astype(F32)
            for a, b in cuts:
                next(outs)[...] = value[a:b, :].astype(kind)

    return call(
        body,
        where,
        inputs,
        specs,
        out_shape,
        20 * MIB,
        scratch=[pltpu.VMEM((half, chunk), F32)],
        name=name,
        estimate=busy(estimate),
    )


def assemble(where, blocks, rows, parts):
    half = blocks[0][2].shape[1]
    inputs = [x for _, _, x in blocks]

    def body(w, *refs):
        out, sems = refs[-2:]
        copies = []
        for n, (s, low, x) in enumerate(blocks):
            size = x.shape[0]
            at = pl.ds(pl.multiple_of((w[0] ^ s) * rows + low, size), size)
            copies.append(pltpu.make_async_copy(refs[n], out.at[at, :], sems.at[n]))
        for copy in copies:
            copy.start()
        for copy in copies:
            copy.wait()

    return pl.pallas_call(
        body,
        out_shape=jax.ShapeDtypeStruct((parts * rows, half), BF16),
        in_specs=[pl.BlockSpec(memory_space=pltpu.SMEM)]
        + [pl.BlockSpec(memory_space=pl.ANY)] * len(inputs),
        out_specs=pl.BlockSpec(memory_space=pl.ANY),
        scratch_shapes=[pltpu.SemaphoreType.DMA((len(inputs),))],
        compiler_params=pltpu.CompilerParams(vmem_limit_bytes=4 * MIB),
        cost_estimate=busy(2),
        name="assemble",
    )(where, *inputs)


def join(where, own, other):
    width, half = own.shape

    def body(w, own_ref, other_ref, out):
        @pl.when(w[1] == 0)
        def _():
            out[:, :half] = own_ref[...]
            out[:, half:] = other_ref[...]

        @pl.when(w[1] != 0)
        def _():
            out[:, :half] = other_ref[...]
            out[:, half:] = own_ref[...]

    return call(
        body,
        where,
        [own, other],
        [whole(own), whole(other)],
        [jax.ShapeDtypeStruct((width, 2 * half), BF16)],
        20 * MIB,
        name="join",
        estimate=busy(1),
    )[0]


def update_step(where, k, pieces, grads, proj, moments, before):
    half, span = grads[0].shape
    rank = CORES * half
    features = moments[0].shape[0]
    width = proj.shape[0]
    rows = min(512, width)
    steps = width // rows
    some = 16

    def piece(w):
        return lax.rem(w[2] + pieces - k, pieces)

    def body(w, own, other, proj_ref, first_ref, second_ref, *refs):
        outs, update = refs[-10:-8], refs[-8]
        moment, grad, ratio, direction, out = refs[-7:-2]
        moment_out, update_out = refs[-2:]
        features_at = pl.ds(pl.multiple_of(piece(w) * span, span), span)
        stores = [
            pltpu.make_async_copy(moment.at[n], outs[n].at[features_at, :], moment_out.at[n])
            for n in range(2)
        ]
        update_stores = [
            pltpu.make_async_copy(
                out.at[pl.ds(r * rows, rows), :],
                update.at[pl.ds(r * rows, rows), features_at],
                update_out.at[r],
            )
            for r in range(steps)
        ]
        for h in range(2):
            grad[:, pl.ds(h * half, half)] = jnp.where(w[1] == h, own[...], other[...]).T
        first_scale = 1.0 / (1.0 - 0.9**STEP)
        second_scale = 1.0 / (1.0 - 0.999**STEP)

        def adam(n, _):
            at = pl.ds(pl.multiple_of(n * some, some), some)
            grad_low = grad[at, :].astype(F32)
            first_new = 0.9 * first_ref[at, :] + 0.1 * grad_low
            second_new = 0.999 * second_ref[at, :] + 0.001 * grad_low * grad_low
            moment[0, at, :] = first_new
            moment[1, at, :] = second_new
            scaled = second_new * second_scale
            root = scaled * lax.rsqrt(scaled)
            ratio[at, :] = ((first_new * first_scale) / (root + 1e-08)).astype(BF16)
            return 0

        lax.fori_loop(0, span // some, adam, 0, unroll=8)
        for copy in stores:
            copy.start()
        direction[...] = ratio[...].T
        for r in range(steps):
            at = pl.ds(r * rows, rows)
            out[at, :] = jnp.dot(proj_ref[at, :], direction[...], preferred_element_type=F32)
            update_stores[r].start()
        for copy in stores + update_stores:
            copy.wait()

    inputs = [*grads, proj, *moments]
    any_space = pl.BlockSpec(memory_space=pl.ANY)
    in_specs = [whole(x) for x in (*grads, proj)]
    in_specs += [pl.BlockSpec((span, rank), lambda i, w: (piece(w), 0))] * 2
    aliases = {}
    if before is not None:
        aliases = {1 + len(inputs) + n: n for n in range(3)}
        inputs += before
        in_specs += [any_space] * 3
    return pl.pallas_call(
        body,
        out_shape=[jax.ShapeDtypeStruct(x.shape, F32) for x in moments]
        + [jax.ShapeDtypeStruct((width, features), F32)],
        grid_spec=pltpu.PrefetchScalarGridSpec(
            num_scalar_prefetch=1,
            grid=(1,),
            in_specs=in_specs,
            out_specs=[any_space] * 3,
            scratch_shapes=[
                pltpu.VMEM((2, span, rank), F32),
                pltpu.VMEM((span, rank), BF16),
                pltpu.VMEM((span, rank), BF16),
                pltpu.VMEM((rank, span), BF16),
                pltpu.VMEM((width, span), F32),
                pltpu.SemaphoreType.DMA((2,)),
                pltpu.SemaphoreType.DMA((steps,)),
            ],
        ),
        input_output_aliases=aliases,
        compiler_params=pltpu.CompilerParams(vmem_limit_bytes=28 * MIB),
        cost_estimate=busy(6),
        name="update_step",
    )(where, *inputs)


def in_vmem(x):
    return pltpu.with_memory_space_constraint(x, pltpu.VMEM)


def after(x, *others):
    return lax.optimization_barrier((x, *others))[0]


def add_up(arrays):
    return functools.reduce(jnp.add, [x.astype(F32) for x in arrays]).astype(BF16)


def on_device(dp, fsdp, acts, cotangent, projector, first_moment, second_moment):
    rows, rank = projector.shape
    half = rank // CORES
    groups = dp // CORES
    pieces = 2 if groups % 2 == 0 else 1
    span = rows // pieces
    chunk = span // 2 if span % 256 == 0 else span
    chunks = range(span // chunk)
    fsdp_at = lax.axis_index("fsdp").astype(jnp.int32)
    dp_at = lax.axis_index("dp")
    core_at = (dp_at % CORES).astype(jnp.int32)
    piece_at = ((dp_at // CORES) % pieces).astype(jnp.int32)
    where = jnp.stack([fsdp_at, core_at, piece_at])

    def to_core(x):
        return lax.ppermute(x, "dp", [(i, i ^ 1) for i in range(dp)])

    def to_fsdp(x, s):
        return lax.ppermute(x, "fsdp", [(i, i ^ s) for i in range(fsdp)])

    def to_piece(x, k):
        pairs = []
        for i in range(dp):
            group, core = divmod(i, CORES)
            base = group - group % pieces
            pairs.append((i, (base + (group + k) % pieces) * CORES + core))
        return lax.ppermute(x, "dp", pairs)

    def to_base(x, k):
        return lax.ppermute(x, "dp", [(i, (i + k * pieces * CORES) % dp) for i in range(dp)])

    def links(s):
        return (s & -s, 1 << (s.bit_length() - 1))

    levels = [
        [s for s in range(fsdp) if s.bit_count() == n] for n in range(fsdp.bit_length())
    ]

    part = rows // 2
    own_half, cot_out = cut_out(
        fsdp_at[None], core_at[None], piece_at[None], projector, cotangent, fsdp, pieces
    )
    held = {0: [(0, 0, own_half)]}
    for level in levels[1:]:
        for s in level:
            if s.bit_count() == 1:
                held[s] = [(s, 0, to_fsdp(own_half, s))]
                continue
            held[s] = []
            for n, link in enumerate(links(s)):
                source = held[s ^ link]
                x = source[n][2] if len(source) > 1 else source[0][2][n * part : (n + 1) * part]
                held[s].append((s, n * part, to_fsdp(x, link)))
    acts_pair = [acts, in_vmem(to_core(acts))]
    cots = [(cotangent, False), (in_vmem(to_core(after(cotangent, own_half))), False)]

    total = None
    for n, level in enumerate(levels):
        entries = [x for s in level for x in held[s]]
        last = n == len(levels) - 1
        total = coords_step(where, acts_pair, entries, total, rows, last, f"coords_{n}")
    full = [(0, half)]
    entries = [(s, 0, 0, [], full) for s in range(fsdp)]
    far_coords = None
    if pieces > 1:
        far_coords = to_piece(total, 1)
    sums = terms_step(
        where, cots, total, entries, pieces, span, span, "terms_chip", F32, 12
    )
    landed = {s: [(0, x)] for s, x in enumerate(sums)}
    cots_far = []
    if pieces > 1:
        arrived = after(to_piece(cot_out, 1), total)
        cots_far = [(arrived, True), (in_vmem(to_core(arrived)), True)]
        entries = [(0, 1, 0, [], full)]
        (pair_sum,) = terms_step(
            where, cots, total, entries, pieces, span, span, "terms_pair"
        )
        landed[0].append((0, to_piece(pair_sum, 1)))

    middle = half // 2
    halves = [(0, middle), (middle, half)]
    for n in range(len(levels) - 1, 1, -1):
        entries = [(s, 0, 0, landed[s], halves) for s in levels[n]]
        outs = iter(
            terms_step(
                where, cots_far, far_coords, entries, pieces, span, span, f"terms_{n}"
            )
        )
        for s in levels[n]:
            for m, link in enumerate(links(s)):
                landed[s ^ link].append((m * middle, to_fsdp(next(outs), link)))
    near = {j: [] for j in chunks}
    if fsdp > 1:
        entries = [(s, 0, j, landed[s], full) for j in chunks for s in levels[1]]
        outs = terms_step(
            where, cots_far, far_coords, entries, pieces, span, chunk, "terms_1"
        )
        for (s, _, j, _, _), x in zip(entries, outs):
            near[j].append((0, to_fsdp(x, s)))
    parts = []
    for j in chunks:
        entries = [(0, 0, j, landed[0] + near[j], full)]
        (x,) = terms_step(where, [], None, entries, pieces, span, chunk, "terms_0", BF16, 1)
        parts.append([x] + [to_base(x, k) for k in range(1, groups // pieces)])

    blocks = [(s, low, after(x, total)) for s in range(fsdp) for s, low, x in held[s]]
    own_proj = assemble(where, blocks, rows, fsdp)
    other_proj = to_core(own_proj)
    proj = join(where, own_proj, after(other_proj, total))
    moments = (first_moment, second_moment)
    parts[0] = [after(x, proj) for x in parts[0]]
    mine = jnp.concatenate([add_up(x) for x in parts], axis=1)
    outputs = update_step(where, 0, pieces, (mine, to_core(mine)), proj, moments, None)
    if pieces > 1:
        others = to_piece(mine, 1)
        pair = (others, to_core(after(others, *outputs)))
        outputs = update_step(where, 1, pieces, pair, proj, moments, outputs)
    return tuple(outputs)


def solution(mesh):
    in_specs = (
        P(("dp", "fsdp"), None),
        P(("dp", "fsdp"), None),
        P("fsdp", None),
        P("fsdp", None),
        P("fsdp", None),
    )
    out_specs = (P("fsdp", None), P("fsdp", None), P(None, "fsdp"))
    body = functools.partial(on_device, mesh.shape["dp"], mesh.shape["fsdp"])
    return jax.shard_map(body, mesh=mesh, in_specs=in_specs, out_specs=out_specs, check_vma=False)
```

```python
import functools

import jax
import jax.numpy as jnp
from jax import lax
from jax.experimental import pallas as pl
from jax.experimental.pallas import tpu as pltpu
from jax.sharding import PartitionSpec as P

STEP = 2
CORES = 2
MIB = 1024 * 1024
BF16 = jnp.bfloat16
F32 = jnp.float32


def cost(flops, bytes_accessed):
    return pl.CostEstimate(flops=flops, bytes_accessed=bytes_accessed, transcendentals=0)


def busy(us):
    return cost(int(us * 1.15e9), 0)


def whole(array):
    zeros = (0,) * array.ndim
    return pl.BlockSpec(array.shape, lambda i, w: zeros)


def call(body, where, inputs, in_specs, out_shape, limit, scratch=(), name=None, estimate=None):
    return pl.pallas_call(
        body,
        out_shape=out_shape,
        grid_spec=pltpu.PrefetchScalarGridSpec(
            num_scalar_prefetch=1,
            grid=(1,),
            in_specs=in_specs,
            out_specs=[whole(x) for x in out_shape],
            scratch_shapes=scratch,
        ),
        compiler_params=pltpu.CompilerParams(vmem_limit_bytes=limit),
        cost_estimate=estimate,
        name=name,
    )(where, *inputs)


def cut_out(fsdp_at, core, piece, projector, cotangent, fsdp, pieces):
    rows, rank = projector.shape
    half = rank // CORES
    tokens, width = cotangent.shape
    span = width // (fsdp * pieces)
    steps = 4

    def body(fsdp_ref, core_ref, piece_ref, proj_ref, cot_ref, proj_out, cot_out, sems):
        copies = []
        for s in range(1, fsdp):
            block = (fsdp_ref[0] ^ s) * pieces + pieces - 1 - piece_ref[0]
            source = cot_ref.at[:, pl.ds(pl.multiple_of(block * span, span), span)]
            copies.append((source, cot_out.at[:, pl.ds((s - 1) * span, span)]))
        columns = pl.ds(pl.multiple_of(core_ref[0] * half, half), half)
        for n in range(steps):
            at = pl.ds(n * (rows // steps), rows // steps)
            copies.append((proj_ref.at[at, columns], proj_out.at[at, :]))
        copies = [pltpu.make_async_copy(x, y, sems.at[n]) for n, (x, y) in enumerate(copies)]
        for copy in copies:
            copy.start()
        for copy in copies:
            copy.wait()

    hbm = [pltpu.with_memory_space_constraint(x, pltpu.HBM) for x in (projector, cotangent)]
    return pl.pallas_call(
        body,
        out_shape=[
            jax.ShapeDtypeStruct((rows, half), BF16),
            jax.ShapeDtypeStruct((tokens, (fsdp - 1) * span), BF16),
        ],
        in_specs=[pl.BlockSpec(memory_space=pltpu.SMEM)] * 3
        + [pl.BlockSpec(memory_space=pl.ANY)] * 2,
        out_specs=[pl.BlockSpec(memory_space=pltpu.VMEM)] * 2,
        scratch_shapes=[pltpu.SemaphoreType.DMA((fsdp + steps,))],
        compiler_params=pltpu.CompilerParams(vmem_limit_bytes=8 * MIB),
        cost_estimate=busy(1),
        name="cut_out",
    )(fsdp_at, core, piece, *hbm)


def coords_step(where, acts, proj, total, rows, last, name):
    tokens = acts[0].shape[0]
    half = proj[0][2].shape[1]
    inputs, specs = [], []
    for s, low, block in proj:
        size = block.shape[0]
        at = functools.partial(
            lambda s, low, size, i, w: (0, ((w[0] ^ s) * rows + low) // size), s, low, size
        )
        inputs += [*acts, block]
        specs += [pl.BlockSpec((tokens, size), at)] * 2 + [whole(block)]
    if total is not None:
        inputs.append(total)
        specs.append(whole(total))
    if last:
        shape = jax.ShapeDtypeStruct((half, 2 * tokens), BF16)
    else:
        shape = jax.ShapeDtypeStruct((2 * tokens, half), F32)

    def body(w, *refs):
        out = refs[len(inputs)]
        for t in range(2):
            span = slice(t * tokens, (t + 1) * tokens)
            value = None if total is None else refs[3 * len(proj)][span, :]
            for n in range(len(proj)):
                part = jnp.dot(
                    refs[3 * n + t][...], refs[3 * n + 2][...], preferred_element_type=F32
                )
                value = part if value is None else value + part
            if last:
                out[:, span] = value.T.astype(BF16)
            else:
                out[span, :] = value

    return call(
        body,
        where,
        inputs,
        specs,
        [shape],
        16 * MIB,
        name=name,
        estimate=busy(8),
    )[0]


def terms_step(where, cots, coords, entries, pieces, span, chunk, name, kind=BF16, estimate=1):
    per_piece = span // chunk
    half = entries[0][4][-1][1]
    inputs = [] if coords is None else [coords]
    specs = [whole(x) for x in inputs]
    out_shape = []
    for s, other, j, added, cuts in entries:
        for x, packed in cots:
            if packed and s == 0:
                continue

            def at(i, w, s=s, other=other, j=j, packed=packed):
                if packed:
                    return (0, (s - 1) * per_piece + j)
                piece = lax.rem(w[2] + other, pieces)
                return (0, ((w[0] ^ s) * pieces + piece) * per_piece + j)

            inputs.append(x)
            specs.append(pl.BlockSpec((x.shape[0], chunk), at))
        for _, x in added:
            column = j if x.shape[1] > chunk else 0
            at = functools.partial(lambda c, i, w: (0, c), column)
            inputs.append(x)
            specs.append(pl.BlockSpec((x.shape[0], chunk), at))
        out_shape += [jax.ShapeDtypeStruct((b - a, chunk), kind) for a, b in cuts]

    def body(w, *refs):
        ins = iter(refs[: len(inputs)])
        outs = iter(refs[len(inputs) : len(inputs) + len(out_shape)])
        value = refs[-1]
        coords_ref = None if coords is None else next(ins)
        for s, _, _, added, cuts in entries:
            term = None
            for n, (x, packed) in enumerate(cots):
                if packed and s == 0:
                    continue
                tokens = x.shape[0]
                part = jnp.dot(
                    coords_ref[:, n * tokens : (n + 1) * tokens],
                    next(ins)[...],
                    preferred_element_type=F32,
                )
                term = part if term is None else term + part
            extra = [(low, x.shape[0], next(ins)) for low, x in added]
            for low, size, ref in extra:
                if size == half:
                    part = ref[...].astype(F32)
                    term = part if term is None else term + part
            value[...] = term
            for low, size, ref in extra:
                if size < half:
                    value[low : low + size, :] += ref[...].astype(F32)
            for a, b in cuts:
                next(outs)[...] = value[a:b, :].astype(kind)

    return call(
        body,
        where,
        inputs,
        specs,
        out_shape,
        20 * MIB,
        scratch=[pltpu.VMEM((half, chunk), F32)],
        name=name,
        estimate=busy(estimate),
    )


def assemble(where, blocks, rows, parts):
    half = blocks[0][2].shape[1]
    inputs = [x for _, _, x in blocks]

    def body(w, *refs):
        out, sems = refs[-2:]
        copies = []
        for n, (s, low, x) in enumerate(blocks):
            size = x.shape[0]
            at = pl.ds(pl.multiple_of((w[0] ^ s) * rows + low, size), size)
            copies.append(pltpu.make_async_copy(refs[n], out.at[at, :], sems.at[n]))
        for copy in copies:
            copy.start()
        for copy in copies:
            copy.wait()

    return pl.pallas_call(
        body,
        out_shape=jax.ShapeDtypeStruct((parts * rows, half), BF16),
        in_specs=[pl.BlockSpec(memory_space=pltpu.SMEM)]
        + [pl.BlockSpec(memory_space=pl.ANY)] * len(inputs),
        out_specs=pl.BlockSpec(memory_space=pl.ANY),
        scratch_shapes=[pltpu.SemaphoreType.DMA((len(inputs),))],
        compiler_params=pltpu.CompilerParams(vmem_limit_bytes=4 * MIB),
        cost_estimate=busy(2),
        name="assemble",
    )(where, *inputs)


def join(where, own, other):
    width, half = own.shape

    def body(w, own_ref, other_ref, out):
        @pl.when(w[1] == 0)
        def _():
            out[:, :half] = own_ref[...]
            out[:, half:] = other_ref[...]

        @pl.when(w[1] != 0)
        def _():
            out[:, :half] = other_ref[...]
            out[:, half:] = own_ref[...]

    return call(
        body,
        where,
        [own, other],
        [whole(own), whole(other)],
        [jax.ShapeDtypeStruct((width, 2 * half), BF16)],
        20 * MIB,
        name="join",
        estimate=busy(1),
    )[0]


def update_step(where, k, pieces, grads, proj, moments, before):
    half, span = grads[0].shape
    rank = CORES * half
    features = moments[0].shape[0]
    width = proj.shape[0]
    rows = min(256, width)
    steps = width // rows
    some = 16

    def piece(w):
        return lax.rem(w[2] + pieces - k, pieces)

    def body(w, own, *refs):
        others, (proj_ref, first_ref, second_ref) = refs[: len(grads) - 1], refs[len(grads) - 1 :][:3]
        outs, update = refs[-10:-8], refs[-8]
        moment, grad, ratio, direction, out = refs[-7:-2]
        moment_out, update_out = refs[-2:]
        features_at = pl.ds(pl.multiple_of(piece(w) * span, span), span)
        stores = [
            pltpu.make_async_copy(moment.at[n], outs[n].at[features_at, :], moment_out.at[n])
            for n in range(2)
        ]
        update_stores = [
            pltpu.make_async_copy(
                out.at[pl.ds(r * rows, rows), :],
                update.at[pl.ds(r * rows, rows), features_at],
                update_out.at[r],
            )
            for r in range(steps)
        ]
        for n, other in enumerate(others):
            size = other.shape[1]
            at = pl.ds(n * size, size)
            for h in range(2):
                part = jnp.where(w[1] == h, own[:, at], other[...])
                grad[at, pl.ds(h * half, half)] = part.T
        first_scale = 1.0 / (1.0 - 0.9**STEP)
        second_scale = 1.0 / (1.0 - 0.999**STEP)

        def adam(n, _):
            at = pl.ds(pl.multiple_of(n * some, some), some)
            grad_low = grad[at, :].astype(F32)
            first_new = 0.9 * first_ref[at, :] + 0.1 * grad_low
            second_new = 0.999 * second_ref[at, :] + 0.001 * grad_low * grad_low
            moment[0, at, :] = first_new
            moment[1, at, :] = second_new
            scaled = second_new * second_scale
            root = scaled * lax.rsqrt(scaled)
            ratio[at, :] = ((first_new * first_scale) / (root + 1e-08)).astype(BF16)
            return 0

        lax.fori_loop(0, span // some, adam, 0, unroll=8)
        for copy in stores:
            copy.start()
        direction[...] = ratio[...].T
        for r in range(steps):
            at = pl.ds(r * rows, rows)
            out[at, :] = jnp.dot(proj_ref[at, :], direction[...], preferred_element_type=F32)
            update_stores[r].start()
        for copy in stores + update_stores:
            copy.wait()

    inputs = [*grads, proj, *moments]
    any_space = pl.BlockSpec(memory_space=pl.ANY)
    in_specs = [whole(x) for x in (*grads, proj)]
    in_specs += [pl.BlockSpec((span, rank), lambda i, w: (piece(w), 0))] * 2
    aliases = {}
    if before is not None:
        aliases = {1 + len(inputs) + n: n for n in range(3)}
        inputs += before
        in_specs += [any_space] * 3
    return pl.pallas_call(
        body,
        out_shape=[jax.ShapeDtypeStruct(x.shape, F32) for x in moments]
        + [jax.ShapeDtypeStruct((width, features), F32)],
        grid_spec=pltpu.PrefetchScalarGridSpec(
            num_scalar_prefetch=1,
            grid=(1,),
            in_specs=in_specs,
            out_specs=[any_space] * 3,
            scratch_shapes=[
                pltpu.VMEM((2, span, rank), F32),
                pltpu.VMEM((span, rank), BF16),
                pltpu.VMEM((span, rank), BF16),
                pltpu.VMEM((rank, span), BF16),
                pltpu.VMEM((width, span), F32),
                pltpu.SemaphoreType.DMA((2,)),
                pltpu.SemaphoreType.DMA((steps,)),
            ],
        ),
        input_output_aliases=aliases,
        compiler_params=pltpu.CompilerParams(vmem_limit_bytes=28 * MIB),
        cost_estimate=busy(0.5),
        name="update_step",
    )(where, *inputs)


def in_vmem(x):
    return pltpu.with_memory_space_constraint(x, pltpu.VMEM)


def after(x, *others):
    return lax.optimization_barrier((x, *others))[0]


def add_up(arrays):
    return functools.reduce(jnp.add, [x.astype(F32) for x in arrays]).astype(BF16)


def on_device(dp, fsdp, acts, cotangent, projector, first_moment, second_moment):
    rows, rank = projector.shape
    half = rank // CORES
    groups = dp // CORES
    pieces = 2 if groups % 2 == 0 else 1
    span = rows // pieces
    chunk = span // 2 if span % 256 == 0 else span
    chunks = range(span // chunk)
    fsdp_at = lax.axis_index("fsdp").astype(jnp.int32)
    dp_at = lax.axis_index("dp")
    core_at = (dp_at % CORES).astype(jnp.int32)
    piece_at = ((dp_at // CORES) % pieces).astype(jnp.int32)
    where = jnp.stack([fsdp_at, core_at, piece_at])

    def to_core(x):
        return lax.ppermute(x, "dp", [(i, i ^ 1) for i in range(dp)])

    def to_fsdp(x, s):
        return lax.ppermute(x, "fsdp", [(i, i ^ s) for i in range(fsdp)])

    def to_piece(x, k):
        pairs = []
        for i in range(dp):
            group, core = divmod(i, CORES)
            base = group - group % pieces
            pairs.append((i, (base + (group + k) % pieces) * CORES + core))
        return lax.ppermute(x, "dp", pairs)

    def to_base(x, k):
        return lax.ppermute(x, "dp", [(i, (i + k * pieces * CORES) % dp) for i in range(dp)])

    def links(s):
        return (s & -s, 1 << (s.bit_length() - 1))

    levels = [
        [s for s in range(fsdp) if s.bit_count() == n] for n in range(fsdp.bit_length())
    ]

    part = rows // 2
    own_half, cot_out = cut_out(
        fsdp_at[None], core_at[None], piece_at[None], projector, cotangent, fsdp, pieces
    )
    held = {0: [(0, 0, own_half)]}
    for level in levels[1:]:
        for s in level:
            if s.bit_count() == 1:
                held[s] = [(s, 0, to_fsdp(own_half, s))]
                continue
            held[s] = []
            for n, link in enumerate(links(s)):
                source = held[s ^ link]
                x = source[n][2] if len(source) > 1 else source[0][2][n * part : (n + 1) * part]
                held[s].append((s, n * part, to_fsdp(x, link)))
    acts_pair = [acts, in_vmem(to_core(acts))]
    cots = [(cotangent, False), (in_vmem(to_core(after(cotangent, own_half))), False)]

    total = None
    for n, level in enumerate(levels):
        entries = [x for s in level for x in held[s]]
        last = n == len(levels) - 1
        total = coords_step(where, acts_pair, entries, total, rows, last, f"coords_{n}")
    full = [(0, half)]
    entries = [(s, 0, 0, [], full) for s in range(fsdp)]
    far_coords = None
    if pieces > 1:
        far_coords = to_piece(total, 1)
    sums = terms_step(
        where, cots, total, entries, pieces, span, span, "terms_chip", F32, 12
    )
    landed = {s: [(0, x)] for s, x in enumerate(sums)}
    cots_far = []
    if pieces > 1:
        arrived = after(to_piece(cot_out, 1), total)
        cots_far = [(arrived, True), (in_vmem(to_core(arrived)), True)]
        entries = [(0, 1, 0, [], full)]
        (pair_sum,) = terms_step(
            where, cots, total, entries, pieces, span, span, "terms_pair"
        )
        landed[0].append((0, to_piece(pair_sum, 1)))

    middle = half // 2
    halves = [(0, middle), (middle, half)]
    for n in range(len(levels) - 1, 1, -1):
        entries = [(s, 0, 0, landed[s], halves) for s in levels[n]]
        outs = iter(
            terms_step(
                where, cots_far, far_coords, entries, pieces, span, span, f"terms_{n}"
            )
        )
        for s in levels[n]:
            for m, link in enumerate(links(s)):
                landed[s ^ link].append((m * middle, to_fsdp(next(outs), link)))
    near = {j: [] for j in chunks}
    if fsdp > 1:
        entries = [(s, 0, j, landed[s], full) for j in chunks for s in levels[1]]
        outs = terms_step(
            where, cots_far, far_coords, entries, pieces, span, chunk, "terms_1"
        )
        for (s, _, j, _, _), x in zip(entries, outs):
            near[j].append((0, to_fsdp(x, s)))
    parts = []
    for j in chunks:
        entries = [(0, 0, j, landed[0] + near[j], full)]
        (x,) = terms_step(where, [], None, entries, pieces, span, chunk, "terms_0", BF16, 1)
        parts.append([x] + [to_base(x, k) for k in range(1, groups // pieces)])

    blocks = [(s, low, after(x, total)) for s in range(fsdp) for s, low, x in held[s]]
    own_proj = assemble(where, blocks, rows, fsdp)
    other_proj = to_core(own_proj)
    proj = join(where, own_proj, after(other_proj, total))
    moments = (first_moment, second_moment)
    parts[0] = [after(x, proj) for x in parts[0]]
    sums_of = [add_up(x) for x in parts]
    mine = jnp.concatenate(sums_of, axis=1)
    others = [to_core(x) for x in sums_of]
    outputs = update_step(where, 0, pieces, (mine, *others), proj, moments, None)
    if pieces > 1:
        others = to_piece(mine, 1)
        pair = (others, to_core(after(others, *outputs)))
        outputs = update_step(where, 1, pieces, pair, proj, moments, outputs)
    return tuple(outputs)


def solution(mesh):
    in_specs = (
        P(("dp", "fsdp"), None),
        P(("dp", "fsdp"), None),
        P("fsdp", None),
        P("fsdp", None),
        P("fsdp", None),
    )
    out_specs = (P("fsdp", None), P("fsdp", None), P(None, "fsdp"))
    body = functools.partial(on_device, mesh.shape["dp"], mesh.shape["fsdp"])
    return jax.shard_map(body, mesh=mesh, in_specs=in_specs, out_specs=out_specs, check_vma=False)
```

```python
import functools

import jax
import jax.numpy as jnp
from jax import lax
from jax.experimental import pallas as pl
from jax.experimental.pallas import tpu as pltpu
from jax.sharding import PartitionSpec as P

STEP = 2
CORES = 2
MIB = 1024 * 1024
BF16 = jnp.bfloat16
F32 = jnp.float32


def cost(flops, bytes_accessed):
    return pl.CostEstimate(flops=flops, bytes_accessed=bytes_accessed, transcendentals=0)


def busy(us):
    return cost(int(us * 1.15e9), 0)


def whole(array):
    zeros = (0,) * array.ndim
    return pl.BlockSpec(array.shape, lambda i, w: zeros)


def call(body, where, inputs, in_specs, out_shape, limit, scratch=(), name=None, estimate=None):
    return pl.pallas_call(
        body,
        out_shape=out_shape,
        grid_spec=pltpu.PrefetchScalarGridSpec(
            num_scalar_prefetch=1,
            grid=(1,),
            in_specs=in_specs,
            out_specs=[whole(x) for x in out_shape],
            scratch_shapes=scratch,
        ),
        compiler_params=pltpu.CompilerParams(vmem_limit_bytes=limit),
        cost_estimate=estimate,
        name=name,
    )(where, *inputs)


def cut_out(fsdp_at, core, piece, projector, cotangent, fsdp, pieces):
    rows, rank = projector.shape
    half = rank // CORES
    tokens, width = cotangent.shape
    span = width // (fsdp * pieces)
    steps = 4

    def body(fsdp_ref, core_ref, piece_ref, proj_ref, cot_ref, proj_out, cot_out, sems):
        copies = []
        for s in range(1, fsdp):
            block = (fsdp_ref[0] ^ s) * pieces + pieces - 1 - piece_ref[0]
            source = cot_ref.at[:, pl.ds(pl.multiple_of(block * span, span), span)]
            copies.append((source, cot_out.at[:, pl.ds((s - 1) * span, span)]))
        columns = pl.ds(pl.multiple_of(core_ref[0] * half, half), half)
        for n in range(steps):
            at = pl.ds(n * (rows // steps), rows // steps)
            copies.append((proj_ref.at[at, columns], proj_out.at[at, :]))
        copies = [pltpu.make_async_copy(x, y, sems.at[n]) for n, (x, y) in enumerate(copies)]
        for copy in copies:
            copy.start()
        for copy in copies:
            copy.wait()

    hbm = [pltpu.with_memory_space_constraint(x, pltpu.HBM) for x in (projector, cotangent)]
    return pl.pallas_call(
        body,
        out_shape=[
            jax.ShapeDtypeStruct((rows, half), BF16),
            jax.ShapeDtypeStruct((tokens, (fsdp - 1) * span), BF16),
        ],
        in_specs=[pl.BlockSpec(memory_space=pltpu.SMEM)] * 3
        + [pl.BlockSpec(memory_space=pl.ANY)] * 2,
        out_specs=[pl.BlockSpec(memory_space=pltpu.VMEM)] * 2,
        scratch_shapes=[pltpu.SemaphoreType.DMA((fsdp + steps,))],
        compiler_params=pltpu.CompilerParams(vmem_limit_bytes=8 * MIB),
        cost_estimate=busy(1),
        name="cut_out",
    )(fsdp_at, core, piece, *hbm)


def coords_step(where, acts, proj, total, rows, last, name):
    tokens = acts[0].shape[0]
    half = proj[0][2].shape[1]
    inputs, specs = [], []
    for s, low, block in proj:
        size = block.shape[0]
        at = functools.partial(
            lambda s, low, size, i, w: (0, ((w[0] ^ s) * rows + low) // size), s, low, size
        )
        inputs += [*acts, block]
        specs += [pl.BlockSpec((tokens, size), at)] * 2 + [whole(block)]
    if total is not None:
        inputs.append(total)
        specs.append(whole(total))
    if last:
        shape = jax.ShapeDtypeStruct((half, 2 * tokens), BF16)
    else:
        shape = jax.ShapeDtypeStruct((2 * tokens, half), F32)

    def body(w, *refs):
        out = refs[len(inputs)]
        for t in range(2):
            span = slice(t * tokens, (t + 1) * tokens)
            value = None if total is None else refs[3 * len(proj)][span, :]
            for n in range(len(proj)):
                part = jnp.dot(
                    refs[3 * n + t][...], refs[3 * n + 2][...], preferred_element_type=F32
                )
                value = part if value is None else value + part
            if last:
                out[:, span] = value.T.astype(BF16)
            else:
                out[span, :] = value

    return call(
        body,
        where,
        inputs,
        specs,
        [shape],
        16 * MIB,
        name=name,
        estimate=busy(8),
    )[0]


def terms_step(where, cots, coords, entries, pieces, span, chunk, name, kind=BF16, estimate=1):
    per_piece = span // chunk
    half = entries[0][4][-1][1]
    inputs = [] if coords is None else [coords]
    specs = [whole(x) for x in inputs]
    out_shape = []
    for s, other, j, added, cuts in entries:
        for x, packed in cots:
            if packed and s == 0:
                continue

            def at(i, w, s=s, other=other, j=j, packed=packed):
                if packed:
                    return (0, (s - 1) * per_piece + j)
                piece = lax.rem(w[2] + other, pieces)
                return (0, ((w[0] ^ s) * pieces + piece) * per_piece + j)

            inputs.append(x)
            specs.append(pl.BlockSpec((x.shape[0], chunk), at))
        for _, x in added:
            column = j if x.shape[1] > chunk else 0
            at = functools.partial(lambda c, i, w: (0, c), column)
            inputs.append(x)
            specs.append(pl.BlockSpec((x.shape[0], chunk), at))
        out_shape += [jax.ShapeDtypeStruct((b - a, chunk), kind) for a, b in cuts]

    def body(w, *refs):
        ins = iter(refs[: len(inputs)])
        outs = iter(refs[len(inputs) : len(inputs) + len(out_shape)])
        value = refs[-1]
        coords_ref = None if coords is None else next(ins)
        for s, _, _, added, cuts in entries:
            term = None
            for n, (x, packed) in enumerate(cots):
                if packed and s == 0:
                    continue
                tokens = x.shape[0]
                part = jnp.dot(
                    coords_ref[:, n * tokens : (n + 1) * tokens],
                    next(ins)[...],
                    preferred_element_type=F32,
                )
                term = part if term is None else term + part
            extra = [(low, x.shape[0], next(ins)) for low, x in added]
            for low, size, ref in extra:
                if size == half:
                    part = ref[...].astype(F32)
                    term = part if term is None else term + part
            value[...] = term
            for low, size, ref in extra:
                if size < half:
                    value[low : low + size, :] += ref[...].astype(F32)
            for a, b in cuts:
                next(outs)[...] = value[a:b, :].astype(kind)

    return call(
        body,
        where,
        inputs,
        specs,
        out_shape,
        20 * MIB,
        scratch=[pltpu.VMEM((half, chunk), F32)],
        name=name,
        estimate=busy(estimate),
    )


def assemble(where, blocks, rows, parts):
    half = blocks[0][2].shape[1]
    inputs = [x for _, _, x in blocks]

    def body(w, *refs):
        out, sems = refs[-2:]
        copies = []
        for n, (s, low, x) in enumerate(blocks):
            size = x.shape[0]
            at = pl.ds(pl.multiple_of((w[0] ^ s) * rows + low, size), size)
            copies.append(pltpu.make_async_copy(refs[n], out.at[at, :], sems.at[n]))
        for copy in copies:
            copy.start()
        for copy in copies:
            copy.wait()

    return pl.pallas_call(
        body,
        out_shape=jax.ShapeDtypeStruct((parts * rows, half), BF16),
        in_specs=[pl.BlockSpec(memory_space=pltpu.SMEM)]
        + [pl.BlockSpec(memory_space=pl.ANY)] * len(inputs),
        out_specs=pl.BlockSpec(memory_space=pl.ANY),
        scratch_shapes=[pltpu.SemaphoreType.DMA((len(inputs),))],
        compiler_params=pltpu.CompilerParams(vmem_limit_bytes=4 * MIB),
        cost_estimate=busy(2),
        name="assemble",
    )(where, *inputs)


def join(where, own, other):
    width, half = own.shape

    def body(w, own_ref, other_ref, out):
        @pl.when(w[1] == 0)
        def _():
            out[:, :half] = own_ref[...]
            out[:, half:] = other_ref[...]

        @pl.when(w[1] != 0)
        def _():
            out[:, :half] = other_ref[...]
            out[:, half:] = own_ref[...]

    return call(
        body,
        where,
        [own, other],
        [whole(own), whole(other)],
        [jax.ShapeDtypeStruct((width, 2 * half), BF16)],
        20 * MIB,
        name="join",
        estimate=busy(1),
    )[0]


def update_step(where, k, pieces, grads, proj, moments, before, written):
    half, span = grads[0].shape
    rank = CORES * half
    features = moments[0].shape[0]
    width = proj.shape[0]
    rows = min(256, width)
    steps = written // rows
    some = 16

    def piece(w):
        return lax.rem(w[2] + pieces - k, pieces)

    def body(w, own, *refs):
        others, (proj_ref, first_ref, second_ref) = refs[: len(grads) - 1], refs[len(grads) - 1 :][:3]
        outs, update, direction = refs[-10:-8], refs[-8], refs[-7]
        moment, grad, ratio, out = refs[-6:-2]
        moment_out, update_out = refs[-2:]
        features_at = pl.ds(pl.multiple_of(piece(w) * span, span), span)
        stores = [
            pltpu.make_async_copy(moment.at[n], outs[n].at[features_at, :], moment_out.at[n])
            for n in range(2)
        ]
        update_stores = [
            pltpu.make_async_copy(
                out.at[pl.ds(r * rows, rows), :],
                update.at[pl.ds(r * rows, rows), features_at],
                update_out.at[r],
            )
            for r in range(steps)
        ]
        for n, other in enumerate(others):
            size = other.shape[1]
            at = pl.ds(n * size, size)
            for h in range(2):
                part = jnp.where(w[1] == h, own[:, at], other[...])
                grad[at, pl.ds(h * half, half)] = part.T
        first_scale = 1.0 / (1.0 - 0.9**STEP)
        second_scale = 1.0 / (1.0 - 0.999**STEP)

        def adam(n, _):
            at = pl.ds(pl.multiple_of(n * some, some), some)
            grad_low = grad[at, :].astype(F32)
            first_new = 0.9 * first_ref[at, :] + 0.1 * grad_low
            second_new = 0.999 * second_ref[at, :] + 0.001 * grad_low * grad_low
            moment[0, at, :] = first_new
            moment[1, at, :] = second_new
            scaled = second_new * second_scale
            root = scaled * lax.rsqrt(scaled)
            ratio[at, :] = ((first_new * first_scale) / (root + 1e-08)).astype(BF16)
            return 0

        lax.fori_loop(0, span // some, adam, 0, unroll=8)
        for copy in stores:
            copy.start()
        direction[...] = ratio[...].T
        for r in range(steps):
            at = pl.ds(r * rows, rows)
            out[at, :] = jnp.dot(proj_ref[at, :], direction[...], preferred_element_type=F32)
            update_stores[r].start()
        for copy in stores + update_stores:
            copy.wait()

    inputs = [*grads, proj, *moments]
    any_space = pl.BlockSpec(memory_space=pl.ANY)
    in_specs = [whole(x) for x in (*grads, proj)]
    in_specs += [pl.BlockSpec((span, rank), lambda i, w: (piece(w), 0))] * 2
    aliases = {}
    if before is not None:
        aliases = {1 + len(inputs) + n: n for n in range(3)}
        inputs += before
        in_specs += [any_space] * 3
    return pl.pallas_call(
        body,
        out_shape=[jax.ShapeDtypeStruct(x.shape, F32) for x in moments]
        + [
            jax.ShapeDtypeStruct((width, features), F32),
            jax.ShapeDtypeStruct((rank, span), BF16),
        ],
        grid_spec=pltpu.PrefetchScalarGridSpec(
            num_scalar_prefetch=1,
            grid=(1,),
            in_specs=in_specs,
            out_specs=[any_space] * 3
            + [pl.BlockSpec((rank, span), lambda i, w: (0, 0))],
            scratch_shapes=[
                pltpu.VMEM((2, span, rank), F32),
                pltpu.VMEM((span, rank), BF16),
                pltpu.VMEM((span, rank), BF16),
                pltpu.VMEM((written, span), F32),
                pltpu.SemaphoreType.DMA((2,)),
                pltpu.SemaphoreType.DMA((steps,)),
            ],
        ),
        input_output_aliases=aliases,
        compiler_params=pltpu.CompilerParams(vmem_limit_bytes=28 * MIB),
        cost_estimate=busy(0.5),
        name="update_step",
    )(where, *inputs)


def expand_rest(where, pieces, direction, proj, update, written):
    rank, span = direction.shape
    width = proj.shape[0]
    rows = min(256, width - written)
    steps = (width - written) // rows

    def body(w, direction_ref, proj_ref, _, update_ref, out, sems):
        features_at = pl.ds(pl.multiple_of(w[2] * span, span), span)
        copies = []
        for r in range(steps):
            at = pl.ds(r * rows, rows)
            there = pl.ds(written + r * rows, rows)
            out[at, :] = jnp.dot(
                proj_ref[there, :], direction_ref[...], preferred_element_type=F32
            )
            copy = pltpu.make_async_copy(
                out.at[at, :], update_ref.at[there, features_at], sems.at[r]
            )
            copy.start()
            copies.append(copy)
        for copy in copies:
            copy.wait()

    any_space = pl.BlockSpec(memory_space=pl.ANY)
    return pl.pallas_call(
        body,
        out_shape=jax.ShapeDtypeStruct(update.shape, F32),
        grid_spec=pltpu.PrefetchScalarGridSpec(
            num_scalar_prefetch=1,
            grid=(1,),
            in_specs=[whole(direction), whole(proj), any_space],
            out_specs=any_space,
            scratch_shapes=[
                pltpu.VMEM((width - written, span), F32),
                pltpu.SemaphoreType.DMA((steps,)),
            ],
        ),
        input_output_aliases={3: 0},
        compiler_params=pltpu.CompilerParams(vmem_limit_bytes=16 * MIB),
        cost_estimate=busy(2),
        name="expand_rest",
    )(where, direction, proj, update)


def in_vmem(x):
    return pltpu.with_memory_space_constraint(x, pltpu.VMEM)


def after(x, *others):
    return lax.optimization_barrier((x, *others))[0]


def add_up(arrays):
    return functools.reduce(jnp.add, [x.astype(F32) for x in arrays]).astype(BF16)


def on_device(dp, fsdp, acts, cotangent, projector, first_moment, second_moment):
    rows, rank = projector.shape
    half = rank // CORES
    groups = dp // CORES
    pieces = 2 if groups % 2 == 0 else 1
    span = rows // pieces
    chunk = span // 2 if span % 256 == 0 else span
    chunks = range(span // chunk)
    fsdp_at = lax.axis_index("fsdp").astype(jnp.int32)
    dp_at = lax.axis_index("dp")
    core_at = (dp_at % CORES).astype(jnp.int32)
    piece_at = ((dp_at // CORES) % pieces).astype(jnp.int32)
    where = jnp.stack([fsdp_at, core_at, piece_at])

    def to_core(x):
        return lax.ppermute(x, "dp", [(i, i ^ 1) for i in range(dp)])

    def to_fsdp(x, s):
        return lax.ppermute(x, "fsdp", [(i, i ^ s) for i in range(fsdp)])

    def to_piece(x, k):
        pairs = []
        for i in range(dp):
            group, core = divmod(i, CORES)
            base = group - group % pieces
            pairs.append((i, (base + (group + k) % pieces) * CORES + core))
        return lax.ppermute(x, "dp", pairs)

    def to_base(x, k):
        return lax.ppermute(x, "dp", [(i, (i + k * pieces * CORES) % dp) for i in range(dp)])

    def links(s):
        return (s & -s, 1 << (s.bit_length() - 1))

    levels = [
        [s for s in range(fsdp) if s.bit_count() == n] for n in range(fsdp.bit_length())
    ]

    part = rows // 2
    own_half, cot_out = cut_out(
        fsdp_at[None], core_at[None], piece_at[None], projector, cotangent, fsdp, pieces
    )
    held = {0: [(0, 0, own_half)]}
    for level in levels[1:]:
        for s in level:
            if s.bit_count() == 1:
                held[s] = [(s, 0, to_fsdp(own_half, s))]
                continue
            held[s] = []
            for n, link in enumerate(links(s)):
                source = held[s ^ link]
                x = source[n][2] if len(source) > 1 else source[0][2][n * part : (n + 1) * part]
                held[s].append((s, n * part, to_fsdp(x, link)))
    acts_pair = [acts, in_vmem(to_core(acts))]
    cots = [(cotangent, False), (in_vmem(to_core(after(cotangent, own_half))), False)]

    total = None
    for n, level in enumerate(levels):
        entries = [x for s in level for x in held[s]]
        last = n == len(levels) - 1
        total = coords_step(where, acts_pair, entries, total, rows, last, f"coords_{n}")
    full = [(0, half)]
    entries = [(s, 0, 0, [], full) for s in range(fsdp)]
    far_coords = None
    if pieces > 1:
        far_coords = to_piece(total, 1)
    sums = terms_step(
        where, cots, total, entries, pieces, span, span, "terms_chip", F32, 12
    )
    landed = {s: [(0, x)] for s, x in enumerate(sums)}
    cots_far = []
    if pieces > 1:
        arrived = after(to_piece(cot_out, 1), total)
        cots_far = [(arrived, True), (in_vmem(to_core(arrived)), True)]
        entries = [(0, 1, 0, [], full)]
        (pair_sum,) = terms_step(
            where, cots, total, entries, pieces, span, span, "terms_pair"
        )
        landed[0].append((0, to_piece(pair_sum, 1)))

    middle = half // 2
    halves = [(0, middle), (middle, half)]
    for n in range(len(levels) - 1, 1, -1):
        entries = [(s, 0, 0, landed[s], halves) for s in levels[n]]
        outs = iter(
            terms_step(
                where, cots_far, far_coords, entries, pieces, span, span, f"terms_{n}"
            )
        )
        for s in levels[n]:
            for m, link in enumerate(links(s)):
                landed[s ^ link].append((m * middle, to_fsdp(next(outs), link)))
    near = {j: [] for j in chunks}
    if fsdp > 1:
        entries = [(s, 0, j, landed[s], full) for j in chunks for s in levels[1]]
        outs = terms_step(
            where, cots_far, far_coords, entries, pieces, span, chunk, "terms_1"
        )
        for (s, _, j, _, _), x in zip(entries, outs):
            near[j].append((0, to_fsdp(x, s)))
    parts = []
    for j in chunks:
        entries = [(0, 0, j, landed[0] + near[j], full)]
        (x,) = terms_step(where, [], None, entries, pieces, span, chunk, "terms_0", BF16, 1)
        parts.append([x] + [to_base(x, k) for k in range(1, groups // pieces)])

    blocks = [(s, low, after(x, total)) for s in range(fsdp) for s, low, x in held[s]]
    own_proj = assemble(where, blocks, rows, fsdp)
    other_proj = to_core(own_proj)
    proj = join(where, own_proj, after(other_proj, total))
    moments = (first_moment, second_moment)
    parts[0] = [after(x, proj) for x in parts[0]]
    sums_of = [add_up(x) for x in parts]
    mine = jnp.concatenate(sums_of, axis=1)
    others = [to_core(x) for x in sums_of]
    width = proj.shape[0]
    written = width * 3 // 4 if pieces > 1 else width
    *outputs, direction = update_step(
        where, 0, pieces, (mine, *others), proj, moments, None, written
    )
    if pieces > 1:
        others = to_piece(mine, 1)
        pair = (others, to_core(after(others, direction)))
        outputs[2] = expand_rest(where, pieces, direction, proj, outputs[2], written)
        *outputs, _ = update_step(where, 1, pieces, pair, proj, moments, outputs, width)
    return tuple(outputs)


def solution(mesh):
    in_specs = (
        P(("dp", "fsdp"), None),
        P(("dp", "fsdp"), None),
        P("fsdp", None),
        P("fsdp", None),
        P("fsdp", None),
    )
    out_specs = (P("fsdp", None), P("fsdp", None), P(None, "fsdp"))
    body = functools.partial(on_device, mesh.shape["dp"], mesh.shape["fsdp"])
    return jax.shard_map(body, mesh=mesh, in_specs=in_specs, out_specs=out_specs, check_vma=False)
```

```python
import functools

import jax
import jax.numpy as jnp
from jax import lax
from jax.experimental import pallas as pl
from jax.experimental.pallas import tpu as pltpu
from jax.sharding import PartitionSpec as P

STEP = 2
CORES = 2
MIB = 1024 * 1024
BF16 = jnp.bfloat16
F32 = jnp.float32


def cost(flops, bytes_accessed):
    return pl.CostEstimate(flops=flops, bytes_accessed=bytes_accessed, transcendentals=0)


def busy(us):
    return cost(int(us * 1.15e9), 0)


def whole(array):
    zeros = (0,) * array.ndim
    return pl.BlockSpec(array.shape, lambda i, w: zeros)


def call(body, where, inputs, in_specs, out_shape, limit, scratch=(), name=None, estimate=None):
    return pl.pallas_call(
        body,
        out_shape=out_shape,
        grid_spec=pltpu.PrefetchScalarGridSpec(
            num_scalar_prefetch=1,
            grid=(1,),
            in_specs=in_specs,
            out_specs=[whole(x) for x in out_shape],
            scratch_shapes=scratch,
        ),
        compiler_params=pltpu.CompilerParams(vmem_limit_bytes=limit),
        cost_estimate=estimate,
        name=name,
    )(where, *inputs)


def cut_out(fsdp_at, core, piece, projector, cotangent, fsdp, pieces):
    rows, rank = projector.shape
    half = rank // CORES
    tokens, width = cotangent.shape
    span = width // (fsdp * pieces)
    steps = 4

    def body(fsdp_ref, core_ref, piece_ref, proj_ref, cot_ref, proj_out, cot_out, sems):
        copies = []
        for s in range(1, fsdp):
            block = (fsdp_ref[0] ^ s) * pieces + pieces - 1 - piece_ref[0]
            source = cot_ref.at[:, pl.ds(pl.multiple_of(block * span, span), span)]
            copies.append((source, cot_out.at[:, pl.ds((s - 1) * span, span)]))
        columns = pl.ds(pl.multiple_of(core_ref[0] * half, half), half)
        for n in range(steps):
            at = pl.ds(n * (rows // steps), rows // steps)
            copies.append((proj_ref.at[at, columns], proj_out.at[at, :]))
        copies = [pltpu.make_async_copy(x, y, sems.at[n]) for n, (x, y) in enumerate(copies)]
        for copy in copies:
            copy.start()
        for copy in copies:
            copy.wait()

    hbm = [pltpu.with_memory_space_constraint(x, pltpu.HBM) for x in (projector, cotangent)]
    return pl.pallas_call(
        body,
        out_shape=[
            jax.ShapeDtypeStruct((rows, half), BF16),
            jax.ShapeDtypeStruct((tokens, (fsdp - 1) * span), BF16),
        ],
        in_specs=[pl.BlockSpec(memory_space=pltpu.SMEM)] * 3
        + [pl.BlockSpec(memory_space=pl.ANY)] * 2,
        out_specs=[pl.BlockSpec(memory_space=pltpu.VMEM)] * 2,
        scratch_shapes=[pltpu.SemaphoreType.DMA((fsdp + steps,))],
        compiler_params=pltpu.CompilerParams(vmem_limit_bytes=8 * MIB),
        cost_estimate=busy(1),
        name="cut_out",
    )(fsdp_at, core, piece, *hbm)


def coords_step(where, acts, proj, total, rows, last, name):
    tokens = acts[0].shape[0]
    half = proj[0][2].shape[1]
    inputs, specs = [], []
    for s, low, block in proj:
        size = block.shape[0]
        at = functools.partial(
            lambda s, low, size, i, w: (0, ((w[0] ^ s) * rows + low) // size), s, low, size
        )
        inputs += [*acts, block]
        specs += [pl.BlockSpec((tokens, size), at)] * 2 + [whole(block)]
    if total is not None:
        inputs.append(total)
        specs.append(whole(total))
    if last:
        shape = jax.ShapeDtypeStruct((half, 2 * tokens), BF16)
    else:
        shape = jax.ShapeDtypeStruct((2 * tokens, half), F32)

    def body(w, *refs):
        out = refs[len(inputs)]
        for t in range(2):
            span = slice(t * tokens, (t + 1) * tokens)
            value = None if total is None else refs[3 * len(proj)][span, :]
            for n in range(len(proj)):
                part = jnp.dot(
                    refs[3 * n + t][...], refs[3 * n + 2][...], preferred_element_type=F32
                )
                value = part if value is None else value + part
            if last:
                out[:, span] = value.T.astype(BF16)
            else:
                out[span, :] = value

    return call(
        body,
        where,
        inputs,
        specs,
        [shape],
        16 * MIB,
        name=name,
        estimate=busy(8),
    )[0]


def terms_step(where, cots, coords, entries, pieces, span, chunk, name, kind=BF16, estimate=1):
    per_piece = span // chunk
    half = entries[0][4][-1][1]
    inputs = [] if coords is None else [coords]
    specs = [whole(x) for x in inputs]
    out_shape = []
    for s, other, j, added, cuts in entries:
        for x, packed in cots:
            if packed and s == 0:
                continue

            def at(i, w, s=s, other=other, j=j, packed=packed):
                if packed:
                    return (0, (s - 1) * per_piece + j)
                piece = lax.rem(w[2] + other, pieces)
                return (0, ((w[0] ^ s) * pieces + piece) * per_piece + j)

            inputs.append(x)
            specs.append(pl.BlockSpec((x.shape[0], chunk), at))
        for _, x in added:
            column = j if x.shape[1] > chunk else 0
            at = functools.partial(lambda c, i, w: (0, c), column)
            inputs.append(x)
            specs.append(pl.BlockSpec((x.shape[0], chunk), at))
        out_shape += [jax.ShapeDtypeStruct((b - a, chunk), kind) for a, b in cuts]

    def body(w, *refs):
        ins = iter(refs[: len(inputs)])
        outs = iter(refs[len(inputs) : len(inputs) + len(out_shape)])
        value = refs[-1]
        coords_ref = None if coords is None else next(ins)
        for s, _, _, added, cuts in entries:
            term = None
            for n, (x, packed) in enumerate(cots):
                if packed and s == 0:
                    continue
                tokens = x.shape[0]
                part = jnp.dot(
                    coords_ref[:, n * tokens : (n + 1) * tokens],
                    next(ins)[...],
                    preferred_element_type=F32,
                )
                term = part if term is None else term + part
            extra = [(low, x.shape[0], next(ins)) for low, x in added]
            for low, size, ref in extra:
                if size == half:
                    part = ref[...].astype(F32)
                    term = part if term is None else term + part
            value[...] = term
            for low, size, ref in extra:
                if size < half:
                    value[low : low + size, :] += ref[...].astype(F32)
            for a, b in cuts:
                next(outs)[...] = value[a:b, :].astype(kind)

    return call(
        body,
        where,
        inputs,
        specs,
        out_shape,
        20 * MIB,
        scratch=[pltpu.VMEM((half, chunk), F32)],
        name=name,
        estimate=busy(estimate),
    )


def assemble(where, blocks, rows, parts):
    half = blocks[0][2].shape[1]
    inputs = [x for _, _, x in blocks]

    def body(w, *refs):
        out, sems = refs[-2:]
        copies = []
        for n, (s, low, x) in enumerate(blocks):
            size = x.shape[0]
            at = pl.ds(pl.multiple_of((w[0] ^ s) * rows + low, size), size)
            copies.append(pltpu.make_async_copy(refs[n], out.at[at, :], sems.at[n]))
        for copy in copies:
            copy.start()
        for copy in copies:
            copy.wait()

    return pl.pallas_call(
        body,
        out_shape=jax.ShapeDtypeStruct((parts * rows, half), BF16),
        in_specs=[pl.BlockSpec(memory_space=pltpu.SMEM)]
        + [pl.BlockSpec(memory_space=pl.ANY)] * len(inputs),
        out_specs=pl.BlockSpec(memory_space=pl.ANY),
        scratch_shapes=[pltpu.SemaphoreType.DMA((len(inputs),))],
        compiler_params=pltpu.CompilerParams(vmem_limit_bytes=4 * MIB),
        cost_estimate=busy(2),
        name="assemble",
    )(where, *inputs)


def join(where, own, other):
    width, half = own.shape

    def body(w, own_ref, other_ref, out):
        @pl.when(w[1] == 0)
        def _():
            out[:, :half] = own_ref[...]
            out[:, half:] = other_ref[...]

        @pl.when(w[1] != 0)
        def _():
            out[:, :half] = other_ref[...]
            out[:, half:] = own_ref[...]

    return call(
        body,
        where,
        [own, other],
        [whole(own), whole(other)],
        [jax.ShapeDtypeStruct((width, 2 * half), BF16)],
        20 * MIB,
        name="join",
        estimate=busy(1),
    )[0]


def update_step(where, k, pieces, grads, proj, moments, before):
    half, span = grads[0].shape
    rank = CORES * half
    features = moments[0].shape[0]
    width = proj.shape[0]
    rows = min(256, width)
    steps = width // rows
    some = 16

    def piece(w):
        return lax.rem(w[2] + pieces - k, pieces)

    def body(w, own, *refs):
        others, (proj_ref, first_ref, second_ref) = refs[: len(grads) - 1], refs[len(grads) - 1 :][:3]
        outs, update = refs[-10:-8], refs[-8]
        moment, grad, ratio, direction, out = refs[-7:-2]
        moment_out, update_out = refs[-2:]
        features_at = pl.ds(pl.multiple_of(piece(w) * span, span), span)
        stores = [
            pltpu.make_async_copy(moment.at[n], outs[n].at[features_at, :], moment_out.at[n])
            for n in range(2)
        ]
        update_stores = [
            pltpu.make_async_copy(
                out.at[pl.ds(r * rows, rows), :],
                update.at[pl.ds(r * rows, rows), features_at],
                update_out.at[r],
            )
            for r in range(steps)
        ]
        for n, other in enumerate(others):
            size = other.shape[1]
            at = pl.ds(n * size, size)
            for h in range(2):
                part = jnp.where(w[1] == h, own[:, at], other[...])
                grad[at, pl.ds(h * half, half)] = part.T
        first_scale = 1.0 / (1.0 - 0.9**STEP)
        second_scale = 1.0 / (1.0 - 0.999**STEP)

        def adam(n, _):
            at = pl.ds(pl.multiple_of(n * some, some), some)
            grad_low = grad[at, :].astype(F32)
            first_new = 0.9 * first_ref[at, :] + 0.1 * grad_low
            second_new = 0.999 * second_ref[at, :] + 0.001 * grad_low * grad_low
            moment[0, at, :] = first_new
            moment[1, at, :] = second_new
            scaled = second_new * second_scale
            root = scaled * lax.rsqrt(scaled)
            ratio[at, :] = ((first_new * first_scale) / (root + 1e-08)).astype(BF16)
            return 0

        lax.fori_loop(0, span // some, adam, 0, unroll=8)
        for copy in stores:
            copy.start()
        direction[...] = ratio[...].T
        for r in range(steps):
            at = pl.ds(r * rows, rows)
            out[at, :] = jnp.dot(proj_ref[at, :], direction[...], preferred_element_type=F32)
            update_stores[r].start()
        for copy in stores + update_stores:
            copy.wait()

    inputs = [*grads, proj, *moments]
    any_space = pl.BlockSpec(memory_space=pl.ANY)
    in_specs = [whole(x) for x in (*grads, proj)]
    in_specs += [pl.BlockSpec((span, rank), lambda i, w: (piece(w), 0))] * 2
    aliases = {}
    if before is not None:
        aliases = {1 + len(inputs) + n: n for n in range(3)}
        inputs += before
        in_specs += [any_space] * 3
    return pl.pallas_call(
        body,
        out_shape=[jax.ShapeDtypeStruct(x.shape, F32) for x in moments]
        + [jax.ShapeDtypeStruct((width, features), F32)],
        grid_spec=pltpu.PrefetchScalarGridSpec(
            num_scalar_prefetch=1,
            grid=(1,),
            in_specs=in_specs,
            out_specs=[any_space] * 3,
            scratch_shapes=[
                pltpu.VMEM((2, span, rank), F32),
                pltpu.VMEM((span, rank), BF16),
                pltpu.VMEM((span, rank), BF16),
                pltpu.VMEM((rank, span), BF16),
                pltpu.VMEM((width, span), F32),
                pltpu.SemaphoreType.DMA((2,)),
                pltpu.SemaphoreType.DMA((steps,)),
            ],
        ),
        input_output_aliases=aliases,
        compiler_params=pltpu.CompilerParams(vmem_limit_bytes=28 * MIB),
        cost_estimate=busy(6),
        name="update_step",
    )(where, *inputs)


def in_vmem(x):
    return pltpu.with_memory_space_constraint(x, pltpu.VMEM)


def after(x, *others):
    return lax.optimization_barrier((x, *others))[0]


def add_up(arrays):
    return functools.reduce(jnp.add, [x.astype(F32) for x in arrays]).astype(BF16)


def on_device(dp, fsdp, acts, cotangent, projector, first_moment, second_moment):
    rows, rank = projector.shape
    half = rank // CORES
    groups = dp // CORES
    pieces = 2 if groups % 2 == 0 else 1
    span = rows // pieces
    chunk = span // 2 if span % 256 == 0 else span
    chunks = range(span // chunk)
    fsdp_at = lax.axis_index("fsdp").astype(jnp.int32)
    dp_at = lax.axis_index("dp")
    core_at = (dp_at % CORES).astype(jnp.int32)
    piece_at = ((dp_at // CORES) % pieces).astype(jnp.int32)
    where = jnp.stack([fsdp_at, core_at, piece_at])

    def to_core(x):
        return lax.ppermute(x, "dp", [(i, i ^ 1) for i in range(dp)])

    def to_fsdp(x, s):
        return lax.ppermute(x, "fsdp", [(i, i ^ s) for i in range(fsdp)])

    def to_piece(x, k):
        pairs = []
        for i in range(dp):
            group, core = divmod(i, CORES)
            base = group - group % pieces
            pairs.append((i, (base + (group + k) % pieces) * CORES + core))
        return lax.ppermute(x, "dp", pairs)

    def to_base(x, k):
        return lax.ppermute(x, "dp", [(i, (i + k * pieces * CORES) % dp) for i in range(dp)])

    def links(s):
        return (s & -s, 1 << (s.bit_length() - 1))

    levels = [
        [s for s in range(fsdp) if s.bit_count() == n] for n in range(fsdp.bit_length())
    ]

    part = rows // 2
    own_half, cot_out = cut_out(
        fsdp_at[None], core_at[None], piece_at[None], projector, cotangent, fsdp, pieces
    )
    held = {0: [(0, 0, own_half)]}
    for level in levels[1:]:
        for s in level:
            if s.bit_count() == 1:
                held[s] = [(s, 0, to_fsdp(own_half, s))]
                continue
            held[s] = []
            for n, link in enumerate(links(s)):
                source = held[s ^ link]
                x = source[n][2] if len(source) > 1 else source[0][2][n * part : (n + 1) * part]
                held[s].append((s, n * part, to_fsdp(x, link)))
    acts_pair = [acts, in_vmem(to_core(acts))]
    cots = [(cotangent, False), (in_vmem(to_core(after(cotangent, own_half))), False)]

    total = None
    for n, level in enumerate(levels):
        entries = [x for s in level for x in held[s]]
        last = n == len(levels) - 1
        total = coords_step(where, acts_pair, entries, total, rows, last, f"coords_{n}")
    full = [(0, half)]
    entries = [(s, 0, 0, [], full) for s in range(fsdp)]
    far_coords = None
    if pieces > 1:
        far_coords = to_piece(total, 1)
    sums = terms_step(
        where, cots, total, entries, pieces, span, span, "terms_chip", F32, 12
    )
    landed = {s: [(0, x)] for s, x in enumerate(sums)}
    cots_far = []
    if pieces > 1:
        arrived = after(to_piece(cot_out, 1), total)
        cots_far = [(arrived, True), (in_vmem(to_core(arrived)), True)]
        entries = [(0, 1, 0, [], full)]
        (pair_sum,) = terms_step(
            where, cots, total, entries, pieces, span, span, "terms_pair"
        )
        landed[0].append((0, to_piece(pair_sum, 1)))

    middle = half // 2
    halves = [(0, middle), (middle, half)]
    for n in range(len(levels) - 1, 1, -1):
        entries = [(s, 0, 0, landed[s], halves) for s in levels[n]]
        outs = iter(
            terms_step(
                where, cots_far, far_coords, entries, pieces, span, span, f"terms_{n}"
            )
        )
        for s in levels[n]:
            for m, link in enumerate(links(s)):
                landed[s ^ link].append((m * middle, to_fsdp(next(outs), link)))
    near = {j: [] for j in chunks}
    if fsdp > 1:
        entries = [(s, 0, j, landed[s], full) for j in chunks for s in levels[1]]
        outs = terms_step(
            where, cots_far, far_coords, entries, pieces, span, chunk, "terms_1"
        )
        for (s, _, j, _, _), x in zip(entries, outs):
            near[j].append((0, to_fsdp(x, s)))
    parts = []
    for j in chunks:
        entries = [(0, 0, j, landed[0] + near[j], full)]
        (x,) = terms_step(where, [], None, entries, pieces, span, chunk, "terms_0", BF16, 1)
        parts.append([x] + [to_base(x, k) for k in range(1, groups // pieces)])

    blocks = [(s, low, after(x, total)) for s in range(fsdp) for s, low, x in held[s]]
    own_proj = assemble(where, blocks, rows, fsdp)
    other_proj = to_core(own_proj)
    proj = join(where, own_proj, after(other_proj, total))
    moments = (first_moment, second_moment)
    parts[0] = [after(x, proj) for x in parts[0]]
    sums_of = [add_up(x) for x in parts]
    mine = jnp.concatenate(sums_of, axis=1)
    others = [to_core(x) for x in sums_of]
    outputs = update_step(where, 0, pieces, (mine, *others), proj, moments, None)
    if pieces > 1:
        others = to_piece(mine, 1)
        pair = (others, to_core(after(others, *outputs)))
        outputs = update_step(where, 1, pieces, pair, proj, moments, outputs)
    return tuple(outputs)


def solution(mesh):
    in_specs = (
        P(("dp", "fsdp"), None),
        P(("dp", "fsdp"), None),
        P("fsdp", None),
        P("fsdp", None),
        P("fsdp", None),
    )
    out_specs = (P("fsdp", None), P("fsdp", None), P(None, "fsdp"))
    body = functools.partial(on_device, mesh.shape["dp"], mesh.shape["fsdp"])
    return jax.shard_map(body, mesh=mesh, in_specs=in_specs, out_specs=out_specs, check_vma=False)
```
